512 devices in a mesh: seq: 128 (over y, z, core), tp: 4 (over x).
Axes of the slice: x: 4, y: 8, z: 8, core: 2. Of those that a mesh axis runs over, the one named last changes fastest.
Arguments:
- proj: bfloat16 [3, 512, 16384], P(None, 'tp', 'seq'), may hold values from -6 to 6
- short_filter: float32 [3, 512, 3], P(None, 'tp'), may hold values from -3.5 to 3.5
- skip_gain: float32 [512], P('tp'), may hold values from -4 to 4
- norm_gain: float32 [512], P('tp'), may hold values from 0.5 to 1.5
- filter_spectrum: float32 [2, 512, 32768], P(None, 'tp', 'seq'), may hold values from -30 to 30, as said below
Outputs:
- output: bfloat16 [512, 16384], P('tp', 'seq')
The draws below stay inside these ranges and needn't reach their ends.
Inputs may be any that keep to these rules, and one draw needn't show every extreme that they name: `filter_spectrum`: real and imaginary parts of a complex filter's transform, of order one to a few, with no symmetry between frequencies k and 32768 - k.
All inputs are finite; a program needn't handle non-finite values.
Results may differ from the reference program's by a relative error of at most 0.008.
Values may be sent and summed in bfloat16 or wider, within the bound.
No kernel may reach another device: no remote copies, remote signals or barrier semaphores. Data moves between devices by JAX's collectives and lax.ppermute only.
A program may use at most 64 MiB of HBM per device.

```python
import jax
import jax.numpy as jnp
from jax import lax

CH = 512
TOKENS = 16384
FFT_LEN = 32768


def draw_filter_spectrum(key, part):
    key = jax.random.fold_in(key, 11)
    key_base = jax.random.fold_in(key, 1)
    key_chan = jax.random.fold_in(key, 2)
    rising = jnp.exp(jnp.log(3.0) * jnp.arange(CH).astype(jnp.float32) / (CH - 1))
    chan_scale = rising * jnp.exp(jax.random.uniform(key_chan, (CH,), jnp.float32, jnp.log(0.6), jnp.log(1.6)))
    base = jnp.clip(jax.random.normal(key_base, (2, CH, FFT_LEN), jnp.float32), -6.0, 6.0)
    return base * chan_scale[None, :, None]


def levels(rng, dims, split, least, largest):
    gain, own = 1.0, jax.random.fold_in(rng, 6)
    for dim, blocks in split:
        heights = jnp.exp(jax.random.uniform(jax.random.fold_in(own, dim), (blocks,), jnp.float32, least / len(split), largest / len(split)))
        gain = gain * jnp.repeat(heights, dims[dim] // blocks).reshape([-1 if axis == dim else 1 for axis in range(len(dims))])
    return gain


def gaussian(stream_key, dims, deviation, bound, cuts=(), dtype=jnp.bfloat16):
    array = jax.random.normal(stream_key, dims, jnp.float32) * deviation
    if len(cuts) > 0:
        array = levels(stream_key, dims, cuts, -0.22, 0.18) * array
    return jnp.clip(array, min=-bound, max=bound).astype(dtype)


def setup_inputs(seed: int = 0) -> dict:
    key_list = jax.random.split(jax.random.key(seed), 6)
    proj = gaussian(key_list[0], (3, CH, TOKENS), 1.0, 6.0, ((1, 4), (2, 128)))
    short_filter = gaussian(key_list[1], (3, CH, 3), 3 ** -0.5, 3.5, ((1, 4),), jnp.float32)
    skip_gain = gaussian(key_list[2], (CH,), 1.0, 4.0, ((0, 4),), jnp.float32)
    norm_gain = jnp.clip(1.0 + 0.1 * jax.random.normal(key_list[3], (CH,), jnp.float32), 0.5, 1.5)
    filter_spectrum = draw_filter_spectrum(jax.random.fold_in(key_list[5], 71), 0)
    return dict(proj=proj, short_filter=short_filter, skip_gain=skip_gain, norm_gain=norm_gain, filter_spectrum=filter_spectrum)


def long_block(pieces):
    signal, spec_re, spec_im = pieces
    spectrum = jnp.fft.fft(signal, n=FFT_LEN, axis=-1)
    filtered = spectrum * lax.complex(spec_re, spec_im)
    back = jnp.fft.ifft(filtered, axis=-1)
    return jnp.real(back)[:, :TOKENS]

def reference(proj, short_filter, skip_gain, norm_gain, filter_spectrum):
    wide = jnp.pad(proj.astype(jnp.float32), ((0, 0), (0, 0), (2, 0)))
    conv = short_filter[:, :, 0:1] * wide[:, :, 2:] + short_filter[:, :, 1:2] * wide[:, :, 1:-1] + short_filter[:, :, 2:3] * wide[:, :, :-2]
    query, keyed, value = (conv[0], conv[1], conv[2])
    mixed = (keyed * value).astype(jnp.bfloat16)
    signal = mixed.astype(jnp.float32).reshape(CH // 8, 8, TOKENS)
    spec_re = filter_spectrum[0].reshape(CH // 8, 8, FFT_LEN)
    spec_im = filter_spectrum[1].reshape(CH // 8, 8, FFT_LEN)
    long_out = lax.map(long_block, (signal, spec_re, spec_im)).reshape(CH, TOKENS)
    pre = query * (long_out + skip_gain[:, None] * mixed.astype(jnp.float32))
    meansq = lax.optimization_barrier(jnp.mean(pre * pre, axis=0))
    return (pre * lax.rsqrt(meansq + 1e-05)[None, :] * norm_gain[:, None]).astype(jnp.bfloat16)
```

```python
import functools

import jax
import jax.numpy as jnp
import numpy as np
from jax import lax
from jax.experimental import pallas as pl
from jax.experimental.pallas import tpu as pltpu
from jax.sharding import PartitionSpec as P

ROWS = 8


def tables(n_coarse, n_fine):
    total = 2 * n_coarse * n_fine
    n1 = np.arange(n_coarse)
    k1 = np.arange(2 * n_coarse)
    n2 = np.arange(n_fine)
    first = 2.0 * np.pi * (np.outer(n1, k1) % (2 * n_coarse)) / (2 * n_coarse)
    edge = np.concatenate([np.cos(first), -np.sin(first)], axis=1)
    inner = 2.0 * np.pi * (np.outer(n2, n2) % n_fine) / n_fine
    w_re, w_im = np.cos(inner), -np.sin(inner)
    fwd = np.block([[w_re, -w_im], [w_im, w_re]])
    inv = np.block([[w_re, w_im], [-w_im, w_re]])
    turn = 2.0 * np.pi * (np.outer(n2, k1) % total) / total
    bf16 = functools.partial(jnp.asarray, dtype=jnp.bfloat16)
    f32 = functools.partial(jnp.asarray, dtype=jnp.float32)
    return bf16(edge), bf16(fwd), bf16(inv), f32(np.cos(turn)), f32(-np.sin(turn))


def pack_kernel(proj_ref, filt_ref, out_ref, wide):
    chans = proj_ref.shape[1]
    lanes = proj_ref.shape[2]
    row = lambda r: pl.ds(r, chans, stride=ROWS)
    for i in range(3):
        wide[row(i), :] = proj_ref[i].astype(jnp.float32)
    for part in range(2):
        for half in range(2):
            wide[row(3 + 2 * part + half), :] = filt_ref[part, :, lanes * half : lanes * (half + 1)]
    wide[row(7), :] = jnp.zeros((chans, lanes), jnp.float32)
    out_ref[...] = wide[...].astype(jnp.bfloat16)


def channel_kernel(
    me_ref, taps_ref, skip_ref, recv_ref, edge_ref, fwd_ref, inv_ref, cos_ref, sin_ref, out_ref, wide
):
    shards = out_ref.shape[0]
    lanes = out_ref.shape[1]
    me = me_ref[0]
    wide[...] = recv_ref[...].astype(jnp.float32)
    plane = lambda r: wide[pl.ds(r, shards, stride=ROWS), :]
    lane = lax.broadcasted_iota(jnp.int32, (shards, lanes), 1)
    shard = lax.broadcasted_iota(jnp.int32, (shards, lanes), 0)

    def delayed(x, steps):
        same = pltpu.roll(x, steps, 1)
        before = jnp.where(shard == 0, 0.0, pltpu.roll(same, 1, 0))
        return jnp.where(lane < steps, before, same)

    def short_conv(i):
        x = plane(i)
        tap = taps_ref[i, pl.ds(me, 1), :]
        return tap[:, 0:1] * x + tap[:, 1:2] * delayed(x, 1) + tap[:, 2:3] * delayed(x, 2)

    query, keyed, value = short_conv(0), short_conv(1), short_conv(2)
    mixed = (keyed * value).astype(jnp.bfloat16)
    dot = functools.partial(lax.dot_general, preferred_element_type=jnp.float32)
    edge = edge_ref[...]
    cos, sin = cos_ref[...], sin_ref[...]
    size = cos.shape[1]
    part = dot(mixed, edge, (((0,), (0,)), ((), ())))
    a_re, a_im = part[:, :size], part[:, size:]
    b = jnp.concatenate([a_re * cos - a_im * sin, a_re * sin + a_im * cos], axis=0)
    spec = dot(fwd_ref[...], b.astype(jnp.bfloat16), (((1,), (0,)), ((), ())))
    s_re, s_im = spec[:lanes], spec[lanes:]
    f_re = jnp.concatenate([plane(3), plane(4)], axis=1)
    f_im = jnp.concatenate([plane(5), plane(6)], axis=1)
    prod = jnp.concatenate([s_re * f_re - s_im * f_im, s_re * f_im + s_im * f_re], axis=0)
    back = dot(inv_ref[...], prod.astype(jnp.bfloat16), (((1,), (0,)), ((), ())))
    c_re, c_im = back[:lanes], back[lanes:]
    d = jnp.concatenate([c_re * cos + c_im * sin, c_im * cos - c_re * sin], axis=1)
    long_out = dot(edge, d.astype(jnp.bfloat16), (((1,), (1,)), ((), ())))
    long_out = long_out * (1.0 / (size * lanes))
    out_ref[...] = query * (long_out + skip_ref[me] * mixed.astype(jnp.float32))


def pack(proj, filter_spectrum):
    chans, lanes = proj.shape[1], proj.shape[2]
    return pl.pallas_call(
        pack_kernel,
        out_shape=jax.ShapeDtypeStruct((chans * ROWS, lanes), jnp.bfloat16),
        scratch_shapes=[pltpu.VMEM((chans * ROWS, lanes), jnp.float32)],
        compiler_params=pltpu.CompilerParams(vmem_limit_bytes=16 * 2**20),
    )(proj, filter_spectrum)


def convolve(me, taps, skip, recv, tabs):
    lanes = recv.shape[1]
    shards = recv.shape[0] // ROWS
    vmem = pl.BlockSpec(memory_space=pltpu.VMEM)
    smem = pl.BlockSpec(memory_space=pltpu.SMEM)
    return pl.pallas_call(
        channel_kernel,
        out_shape=jax.ShapeDtypeStruct((shards, lanes), jnp.float32),
        in_specs=[smem, vmem, smem, vmem] + [vmem] * len(tabs),
        out_specs=vmem,
        scratch_shapes=[pltpu.VMEM((shards * ROWS, lanes), jnp.float32)],
        compiler_params=pltpu.CompilerParams(vmem_limit_bytes=16 * 2**20),
    )(me, taps, skip, recv, *tabs)


def per_device(proj, short_filter, skip_gain, norm_gain, filter_spectrum):
    chans, tok = proj.shape[1], proj.shape[2]
    peers = lax.axis_size("seq")
    groups = lax.axis_size("tp")
    me = lax.axis_index("seq").astype(jnp.int32).reshape(1)
    tabs = tables(peers, tok)
    sent = pack(proj, filter_spectrum).reshape(peers, ROWS, tok)
    recv = lax.all_to_all(sent, "seq", split_axis=0, concat_axis=0, tiled=True)
    pre = convolve(me, short_filter, skip_gain, recv.reshape(peers * ROWS, tok), tabs)
    pre = lax.all_to_all(
        pre.reshape(peers, 1, tok), "seq", split_axis=0, concat_axis=0, tiled=True
    ).reshape(chans, tok)
    meansq = lax.psum(jnp.sum(pre * pre, axis=0), "tp") / (chans * groups)
    return (pre * lax.rsqrt(meansq + 1e-05)[None, :] * norm_gain[:, None]).astype(jnp.bfloat16)


def solution(mesh):
    return jax.shard_map(
        per_device,
        mesh=mesh,
        in_specs=(
            P(None, "tp", "seq"),
            P(None, "tp", None),
            P("tp"),
            P("tp"),
            P(None, "tp", "seq"),
        ),
        out_specs=P("tp", "seq"),
        check_vma=False,
    )
```

```python
import functools

import jax
import jax.numpy as jnp
import numpy as np
from jax import lax
from jax.experimental import pallas as pl
from jax.experimental.pallas import tpu as pltpu
from jax.sharding import PartitionSpec as P

ROWS = 8
CHUNKS = 4


def tables(n_coarse, n_fine):
    total = 2 * n_coarse * n_fine
    n1 = np.arange(n_coarse)
    k1 = np.arange(2 * n_coarse)
    n2 = np.arange(n_fine)
    first = 2.0 * np.pi * (np.outer(n1, k1) % (2 * n_coarse)) / (2 * n_coarse)
    edge = np.concatenate([np.cos(first), -np.sin(first)], axis=1)
    inner = 2.0 * np.pi * (np.outer(n2, n2) % n_fine) / n_fine
    w_re, w_im = np.cos(inner), -np.sin(inner)
    inner = np.concatenate([w_re, w_im], axis=1)
    half = n_fine // 2
    turn = 2.0 * np.pi * (np.outer(n2, k1) % total) / total
    turns = np.concatenate([np.cos(turn), -np.sin(turn)], axis=1)
    coarse = turns.astype(jnp.bfloat16).astype(np.float64)
    rows = [edge, np.concatenate([inner[:half], inner[half:]], axis=1), coarse, turns - coarse]
    return jnp.asarray(np.concatenate(rows, axis=0), jnp.bfloat16)


def pack_kernel(
    proj_hbm, filt_hbm, taps_hbm, skip_hbm, gain_hbm, out_hbm,
    proj_ref, filt_ref, taps_ref, skip_ref, gain_ref, wide, out_ref, sem_in, sem_out, sem_small
):
    chans = proj_ref.shape[1]
    lanes = proj_ref.shape[2]
    size = chans // CHUNKS
    small = [
        pltpu.make_async_copy(taps_hbm, taps_ref, sem_small.at[0]),
        pltpu.make_async_copy(skip_hbm, skip_ref, sem_small.at[1]),
        pltpu.make_async_copy(gain_hbm, gain_ref, sem_small.at[2]),
    ]
    for copy in small:
        copy.start()
    loads = []
    for chunk in range(CHUNKS):
        part = pl.ds(chunk * size, size)
        loads.append([
            pltpu.make_async_copy(proj_hbm.at[:, part], proj_ref.at[:, part], sem_in.at[0, chunk]),
            pltpu.make_async_copy(filt_hbm.at[:, part], filt_ref.at[:, part], sem_in.at[1, chunk]),
        ])
        for copy in loads[-1]:
            copy.start()
    for copy in small:
        copy.wait()
    me = lax.axis_index("seq")
    lane = lax.broadcasted_iota(jnp.int32, (1, lanes), 1)
    own_row = jnp.zeros((1, lanes), jnp.float32)
    planes = [taps_ref[i, m : m + 1, :] for i in range(3) for m in range(3)]
    for p, values in enumerate(planes + [skip_ref[...], gain_ref[...]]):
        own = jnp.sum(jnp.where(lane == me, values, 0.0), axis=1, keepdims=True)
        for k in range(3):
            piece = own.astype(jnp.bfloat16).astype(jnp.float32)
            own_row = jnp.where(lane == 16 * k + p, piece, own_row)
            own = own - piece
    stores = []
    for chunk in range(CHUNKS):
        for copy in loads[chunk]:
            copy.wait()
        base = chunk * size
        rows = pl.ds(base * ROWS, size * ROWS)
        row = lambda r: pl.ds(base * ROWS + r, size, stride=ROWS)
        for i in range(3):
            wide[row(i), :] = proj_ref[i, base : base + size].astype(jnp.float32)
        for part in range(2):
            for half in range(2):
                wide[row(3 + 2 * part + half), :] = filt_ref[
                    part, base : base + size, lanes * half : lanes * (half + 1)
                ]
        wide[row(7), :] = jnp.broadcast_to(own_row, (size, lanes))
        out_ref[rows, :] = wide[rows, :].astype(jnp.bfloat16)
        stores.append(pltpu.make_async_copy(out_ref.at[rows], out_hbm.at[rows], sem_out.at[chunk]))
        stores[-1].start()
    for copy in stores:
        copy.wait()


def channel_kernel(
    recv_ref, waves_ref, out_ref, gain_ref, wide
):
    shards = out_ref.shape[0]
    lanes = out_ref.shape[1]
    wide[...] = recv_ref[...].astype(jnp.float32)
    plane = lambda r: wide[pl.ds(r, shards, stride=ROWS), :]
    me = lax.axis_index("seq")
    merge = lambda x: x + pltpu.roll(x, lanes - 16, 1) + pltpu.roll(x, lanes - 32, 1)
    gain_ref[...] = jnp.broadcast_to(merge(plane(7))[:, 10:11], (shards, lanes))
    own = merge(wide[pl.ds(me * ROWS, ROWS), :][7:8, :])
    param = lambda p: jnp.broadcast_to(own[:, p : p + 1], (1, lanes))
    lane = lax.broadcasted_iota(jnp.int32, (shards, lanes), 1)
    shard = lax.broadcasted_iota(jnp.int32, (shards, lanes), 0)

    def delayed(x, steps):
        same = pltpu.roll(x, steps, 1)
        before = jnp.where(shard == 0, 0.0, pltpu.roll(same, 1, 0))
        return jnp.where(lane < steps, before, same)

    def short_conv(i):
        x = plane(i)
        tap = lambda m: param(3 * i + m)
        return tap(0) * x + tap(1) * delayed(x, 1) + tap(2) * delayed(x, 2)

    query, keyed, value = short_conv(0), short_conv(1), short_conv(2)
    mixed = (keyed * value).astype(jnp.bfloat16)
    dot = functools.partial(lax.dot_general, preferred_element_type=jnp.float32)
    size = 2 * shards
    edge = waves_ref[:shards, :]
    at = shards + lanes // 2
    inner = waves_ref[shards:at, :]
    inner = jnp.concatenate([inner[:, : 2 * lanes], inner[:, 2 * lanes :]], axis=0)
    w_re, w_im = inner[:, :lanes], inner[:, lanes:]
    square = lambda a, b, c, d: jnp.concatenate(
        [jnp.concatenate([a, b], axis=1), jnp.concatenate([c, d], axis=1)], axis=0
    )
    fwd, inv = square(w_re, -w_im, w_im, w_re), square(w_re, w_im, -w_im, w_re)
    turns = waves_ref[at : at + lanes, :].astype(jnp.float32)
    turns = turns + waves_ref[at + lanes :, :].astype(jnp.float32)
    cos, sin = turns[:, :size], turns[:, size:]
    part = dot(mixed, edge, (((0,), (0,)), ((), ())))
    a_re, a_im = part[:, :size], part[:, size:]
    b = jnp.concatenate([a_re * cos - a_im * sin, a_re * sin + a_im * cos], axis=0)
    spec = dot(fwd, b.astype(jnp.bfloat16), (((1,), (0,)), ((), ())))
    s_re, s_im = spec[:lanes], spec[lanes:]
    f_re = jnp.concatenate([plane(3), plane(4)], axis=1)
    f_im = jnp.concatenate([plane(5), plane(6)], axis=1)
    prod = jnp.concatenate([s_re * f_re - s_im * f_im, s_re * f_im + s_im * f_re], axis=0)
    back = dot(inv, prod.astype(jnp.bfloat16), (((1,), (0,)), ((), ())))
    c_re, c_im = back[:lanes], back[lanes:]
    d = jnp.concatenate([c_re * cos + c_im * sin, c_im * cos - c_re * sin], axis=1)
    long_out = dot(edge, d.astype(jnp.bfloat16), (((1,), (1,)), ((), ())))
    long_out = long_out * (1.0 / (size * lanes))
    out_ref[...] = query * (long_out + param(9) * mixed.astype(jnp.float32))


def pack(proj, filter_spectrum, taps, skip, gain):
    chans, lanes = proj.shape[1], proj.shape[2]
    hbm = pl.BlockSpec(memory_space=pltpu.HBM)
    inputs = (proj, filter_spectrum, taps, skip, gain)
    return pl.pallas_call(
        pack_kernel,
        out_shape=jax.ShapeDtypeStruct((chans * ROWS, lanes), jnp.bfloat16),
        in_specs=[hbm] * len(inputs),
        out_specs=hbm,
        scratch_shapes=[pltpu.VMEM(x.shape, x.dtype) for x in inputs]
        + [
            pltpu.VMEM((chans * ROWS, lanes), jnp.float32),
            pltpu.VMEM((chans * ROWS, lanes), jnp.bfloat16),
            pltpu.SemaphoreType.DMA((2, CHUNKS)),
            pltpu.SemaphoreType.DMA((CHUNKS,)),
            pltpu.SemaphoreType.DMA((3,)),
        ],
        compiler_params=pltpu.CompilerParams(vmem_limit_bytes=64 * 2**20),
    )(*inputs)


def convolve(recv, waves):
    lanes = recv.shape[1]
    shards = recv.shape[0] // ROWS
    vmem = pl.BlockSpec(memory_space=pltpu.VMEM)
    return pl.pallas_call(
        channel_kernel,
        out_shape=(jax.ShapeDtypeStruct((shards, lanes), jnp.float32),) * 2,
        in_specs=[vmem] * 2,
        out_specs=(vmem,) * 2,
        scratch_shapes=[pltpu.VMEM((shards * ROWS, lanes), jnp.float32)],
        compiler_params=pltpu.CompilerParams(vmem_limit_bytes=16 * 2**20),
    )(recv, waves)


def per_device(proj, short_filter, skip_gain, norm_gain, filter_spectrum):
    chans, tok = proj.shape[1], proj.shape[2]
    peers = lax.axis_size("seq")
    groups = lax.axis_size("tp")
    waves = tables(peers, tok)
    taps = jnp.swapaxes(short_filter, 1, 2)
    sent = pack(proj, filter_spectrum, taps, skip_gain[None], norm_gain[None])
    recv = lax.all_to_all(
        sent.reshape(peers, ROWS, tok), "seq", split_axis=0, concat_axis=0, tiled=True
    )
    pre, gain = convolve(recv.reshape(peers * ROWS, tok), waves)
    pre = lax.all_to_all(
        pre.reshape(peers, 1, tok), "seq", split_axis=0, concat_axis=0, tiled=True
    ).reshape(chans, tok)
    meansq = lax.psum(jnp.sum(pre * pre, axis=0), "tp") / (chans * groups)
    return (pre * lax.rsqrt(meansq + 1e-05)[None, :] * gain).astype(jnp.bfloat16)


def solution(mesh):
    return jax.shard_map(
        per_device,
        mesh=mesh,
        in_specs=(
            P(None, "tp", "seq"),
            P(None, "tp", None),
            P("tp"),
            P("tp"),
            P(None, "tp", "seq"),
        ),
        out_specs=P("tp", "seq"),
        check_vma=False,
    )
```

```python
import functools

import jax
import jax.numpy as jnp
import numpy as np
from jax import lax
from jax.experimental import pallas as pl
from jax.experimental.pallas import tpu as pltpu
from jax.sharding import PartitionSpec as P

ROWS = 8
CHUNKS = 4


def tables(n_coarse, n_fine):
    total = 2 * n_coarse * n_fine
    n1 = np.arange(n_coarse)
    k1 = np.arange(2 * n_coarse)
    n2 = np.arange(n_fine)
    turn = 2.0 * np.pi * (np.outer(n2, k1) % total) / total
    first = 2.0 * np.pi * (np.outer(n1, k1[:n_coarse]) % (2 * n_coarse)) / (2 * n_coarse)
    edge = np.concatenate([np.cos(first), -np.sin(first)], axis=1)
    inner = 2.0 * np.pi * (np.outer(n2, n2) % n_fine) / n_fine
    inner = np.concatenate([np.cos(inner), -np.sin(inner)], axis=1)
    fold = lambda x: np.concatenate([x[: len(x) // 2], x[len(x) // 2 :]], axis=1)
    turns = np.concatenate([np.cos(turn), -np.sin(turn)], axis=1)
    rows = [fold(edge), fold(inner), turns]
    return jnp.asarray(np.concatenate(rows, axis=0), jnp.bfloat16)


def pack_kernel(
    proj_hbm, filt_hbm, taps_hbm, skip_hbm, gain_hbm, out_ref,
    proj_ref, filt_ref, taps_ref, skip_ref, gain_ref, wide, sem_in, sem_small
):
    chans = proj_ref.shape[1]
    lanes = proj_ref.shape[2]
    size = chans // CHUNKS
    small = [
        pltpu.make_async_copy(taps_hbm, taps_ref, sem_small.at[0]),
        pltpu.make_async_copy(skip_hbm, skip_ref, sem_small.at[1]),
        pltpu.make_async_copy(gain_hbm, gain_ref, sem_small.at[2]),
    ]
    for copy in small:
        copy.start()
    loads = []
    for chunk in range(CHUNKS):
        part = pl.ds(chunk * size, size)
        loads.append([
            pltpu.make_async_copy(proj_hbm.at[:, part], proj_ref.at[:, part], sem_in.at[0, chunk]),
            pltpu.make_async_copy(filt_hbm.at[:, part], filt_ref.at[:, part], sem_in.at[1, chunk]),
        ])
        for copy in loads[-1]:
            copy.start()
    for copy in small:
        copy.wait()
    me = lax.axis_index("seq")
    lane = lax.broadcasted_iota(jnp.int32, (1, lanes), 1)
    own_row = jnp.zeros((1, lanes), jnp.float32)
    planes = [taps_ref[i, m : m + 1, :] for i in range(3) for m in range(3)]
    for p, values in enumerate(planes + [skip_ref[...], gain_ref[...]]):
        own = jnp.sum(jnp.where(lane == me, values, 0.0), axis=1, keepdims=True)
        for k in range(3):
            piece = own.astype(jnp.bfloat16).astype(jnp.float32)
            own_row = jnp.where(lane == 16 * k + p, piece, own_row)
            own = own - piece
    for chunk in range(CHUNKS):
        for copy in loads[chunk]:
            copy.wait()
        base = chunk * size
        rows = pl.ds(base * ROWS, size * ROWS)
        row = lambda r: pl.ds(base * ROWS + r, size, stride=ROWS)
        for i in range(3):
            wide[row(i), :] = proj_ref[i, base : base + size].astype(jnp.float32)
        for part in range(2):
            for half in range(2):
                wide[row(3 + 2 * part + half), :] = filt_ref[
                    part, base : base + size, lanes * half : lanes * (half + 1)
                ]
        wide[row(7), :] = jnp.broadcast_to(own_row, (size, lanes))
        out_ref[rows, :] = wide[rows, :].astype(jnp.bfloat16)


def channel_kernel(
    recv_ref, waves_ref, out_ref, gain_ref, wide
):
    shards = out_ref.shape[0]
    lanes = out_ref.shape[1]
    wide[...] = recv_ref[...].astype(jnp.float32)
    plane = lambda r: wide[pl.ds(r, shards, stride=ROWS), :]
    me = lax.axis_index("seq")
    merge = lambda x: x + pltpu.roll(x, lanes - 16, 1) + pltpu.roll(x, lanes - 32, 1)
    gain_ref[...] = jnp.broadcast_to(merge(plane(7))[:, 10:11], (shards, lanes))
    own = merge(wide[pl.ds(me * ROWS, ROWS), :][7:8, :])
    param = lambda p: jnp.broadcast_to(own[:, p : p + 1], (1, lanes))
    lane = lax.broadcasted_iota(jnp.int32, (shards, lanes), 1)
    shard = lax.broadcasted_iota(jnp.int32, (shards, lanes), 0)

    def delayed(x, steps):
        same = pltpu.roll(x, steps, 1)
        before = jnp.where(shard == 0, 0.0, pltpu.roll(same, 1, 0))
        return jnp.where(lane < steps, before, same)

    def short_conv(i):
        x = plane(i)
        tap = lambda m: param(3 * i + m)
        return tap(0) * x + tap(1) * delayed(x, 1) + tap(2) * delayed(x, 2)

    query, keyed, value = short_conv(0), short_conv(1), short_conv(2)
    mixed = (keyed * value).astype(jnp.bfloat16)
    dot = functools.partial(lax.dot_general, preferred_element_type=jnp.float32)
    size = 2 * shards
    unfold = lambda x: jnp.concatenate([x[:, :size], x[:, size:]], axis=0)
    half = shards // 2
    edge = unfold(waves_ref[:half, :])
    flip = jnp.where(shard % 2 == 0, 1.0, -1.0).astype(jnp.bfloat16)
    c, d = edge[:, :shards], edge[:, shards:]
    edge = jnp.concatenate([c, c * flip, d, d * flip], axis=1)
    inner = unfold(waves_ref[half : half + lanes // 2, :])
    w_re, w_im = inner[:, :lanes], inner[:, lanes:]
    square = lambda a, b, c, d: jnp.concatenate(
        [jnp.concatenate([a, b], axis=1), jnp.concatenate([c, d], axis=1)], axis=0
    )
    fwd, inv = square(w_re, -w_im, w_im, w_re), square(w_re, w_im, -w_im, w_re)
    turns = waves_ref[half + lanes // 2 :, :].astype(jnp.float32)
    cos, sin = turns[:, :size], turns[:, size:]
    part = dot(mixed, edge, (((0,), (0,)), ((), ())))
    a_re, a_im = part[:, :size], part[:, size:]
    b = jnp.concatenate([a_re * cos - a_im * sin, a_re * sin + a_im * cos], axis=0)
    spec = dot(fwd, b.astype(jnp.bfloat16), (((1,), (0,)), ((), ())))
    s_re, s_im = spec[:lanes], spec[lanes:]
    f_re = jnp.concatenate([plane(3), plane(4)], axis=1)
    f_im = jnp.concatenate([plane(5), plane(6)], axis=1)
    prod = jnp.concatenate([s_re * f_re - s_im * f_im, s_re * f_im + s_im * f_re], axis=0)
    back = dot(inv, prod.astype(jnp.bfloat16), (((1,), (0,)), ((), ())))
    c_re, c_im = back[:lanes], back[lanes:]
    d = jnp.concatenate([c_re * cos + c_im * sin, c_im * cos - c_re * sin], axis=1)
    long_out = dot(edge, d.astype(jnp.bfloat16), (((1,), (1,)), ((), ())))
    long_out = long_out * (1.0 / (size * lanes))
    out_ref[...] = query * (long_out + param(9) * mixed.astype(jnp.float32))


def pack(proj, filter_spectrum, taps, skip, gain):
    chans, lanes = proj.shape[1], proj.shape[2]
    hbm = pl.BlockSpec(memory_space=pltpu.HBM)
    inputs = (proj, filter_spectrum, taps, skip, gain)
    return pl.pallas_call(
        pack_kernel,
        out_shape=jax.ShapeDtypeStruct((chans * ROWS, lanes), jnp.bfloat16),
        in_specs=[hbm] * len(inputs),
        out_specs=pl.BlockSpec(memory_space=pltpu.VMEM),
        scratch_shapes=[pltpu.VMEM(x.shape, x.dtype) for x in inputs]
        + [
            pltpu.VMEM((chans * ROWS, lanes), jnp.float32),
            pltpu.SemaphoreType.DMA((2, CHUNKS)),
            pltpu.SemaphoreType.DMA((3,)),
        ],
        compiler_params=pltpu.CompilerParams(vmem_limit_bytes=16 * 2**20),
    )(*(pltpu.with_memory_space_constraint(x, pltpu.HBM) for x in inputs))


def convolve(recv, waves):
    lanes = recv.shape[1]
    shards = recv.shape[0] // ROWS
    vmem = pl.BlockSpec(memory_space=pltpu.VMEM)
    return pl.pallas_call(
        channel_kernel,
        out_shape=(jax.ShapeDtypeStruct((shards, lanes), jnp.float32),) * 2,
        in_specs=[vmem] * 2,
        out_specs=(vmem,) * 2,
        scratch_shapes=[pltpu.VMEM((shards * ROWS, lanes), jnp.float32)],
        compiler_params=pltpu.CompilerParams(vmem_limit_bytes=16 * 2**20),
    )(recv, waves)


def per_device(proj, short_filter, skip_gain, norm_gain, filter_spectrum):
    chans, tok = proj.shape[1], proj.shape[2]
    peers = lax.axis_size("seq")
    groups = lax.axis_size("tp")
    waves = tables(peers, tok)
    taps = jnp.swapaxes(short_filter, 1, 2)
    sent = pack(proj, filter_spectrum, taps, skip_gain[None], norm_gain[None])
    recv = lax.all_to_all(
        sent.reshape(peers, ROWS, tok), "seq", split_axis=0, concat_axis=0, tiled=True
    )
    pre, gain = convolve(recv.reshape(peers * ROWS, tok), waves)
    pre = lax.all_to_all(
        pre.reshape(peers, 1, tok), "seq", split_axis=0, concat_axis=0, tiled=True
    ).reshape(chans, tok)
    squares = jnp.broadcast_to(jnp.sum(pre * pre, axis=0)[None, None], (groups, 1, tok))
    squares = lax.all_to_all(squares, "tp", split_axis=0, concat_axis=0, tiled=True)
    meansq = jnp.sum(squares[:, 0], axis=0) / (chans * groups)
    return (pre * lax.rsqrt(meansq + 1e-05)[None, :] * gain).astype(jnp.bfloat16)


def solution(mesh):
    return jax.shard_map(
        per_device,
        mesh=mesh,
        in_specs=(
            P(None, "tp", "seq"),
            P(None, "tp", None),
            P("tp"),
            P("tp"),
            P(None, "tp", "seq"),
        ),
        out_specs=P("tp", "seq"),
        check_vma=False,
    )
```

```python
import jax
import jax.numpy as jnp
import numpy as np
from jax import lax
from jax.experimental import pallas as pl
from jax.experimental.pallas import tpu as pltpu
from jax.sharding import PartitionSpec as P

ROWS = 6
EDGE_ROW = 5
CHUNKS = 2
PARAMS = 32


def tables(n_coarse, n_fine):
    total = 2 * n_coarse * n_fine
    n1 = np.arange(n_coarse)
    k1 = np.arange(2 * n_coarse)
    n2 = np.arange(n_fine)
    turn = 2.0 * np.pi * (np.outer(n2, k1) % total) / total
    first = 2.0 * np.pi * (np.outer(n1, k1[:n_coarse]) % (2 * n_coarse)) / (2 * n_coarse)
    edge = np.concatenate([np.cos(first), -np.sin(first)], axis=1)
    inner = 2.0 * np.pi * (np.outer(n2, n2) % n_fine) / n_fine
    inner = np.concatenate([np.cos(inner), -np.sin(inner)], axis=1)
    fold = lambda x: np.concatenate([x[: len(x) // 2], x[len(x) // 2 :]], axis=1)
    turns = np.concatenate([np.cos(turn), -np.sin(turn)], axis=1)
    rows = [fold(edge), fold(inner), turns]
    return jnp.asarray(np.concatenate(rows, axis=0), jnp.bfloat16)


def pack_kernel(
    proj_hbm, filt_hbm, taps_hbm, skip_hbm, gain_hbm, out_ref, factor_ref,
    proj_ref, filt_ref, small_ref, wide, sem_in, sem_small
):
    chans = proj_ref.shape[1]
    lanes = proj_ref.shape[2]
    size = chans // CHUNKS
    small = [
        pltpu.make_async_copy(taps_hbm.at[i], small_ref.at[pl.ds(3 * i, 3)], sem_small.at[i])
        for i in range(3)
    ] + [
        pltpu.make_async_copy(skip_hbm, small_ref.at[pl.ds(9, 1)], sem_small.at[3]),
        pltpu.make_async_copy(gain_hbm, small_ref.at[pl.ds(10, 1)], sem_small.at[4]),
    ]
    for copy in small:
        copy.start()
    loads = []
    for chunk in range(CHUNKS):
        part = pl.ds(chunk * size, size)
        loads.append([
            pltpu.make_async_copy(proj_hbm.at[:, part], proj_ref.at[:, part], sem_in.at[0, chunk]),
            pltpu.make_async_copy(filt_hbm.at[:, part], filt_ref.at[:, part], sem_in.at[1, chunk]),
        ])
        for copy in loads[-1]:
            copy.start()
    for copy in small:
        copy.wait()
    me = lax.axis_index("seq")
    lane = lax.broadcasted_iota(jnp.int32, (16, lanes), 1)
    param = lax.broadcasted_iota(jnp.int32, (16, lanes), 0)
    params = jnp.where(param < 11, small_ref[...], 0.0)
    columns = params.T
    own = jnp.sum(jnp.where(lane == me, params, 0.0), axis=1, keepdims=True)
    spread = jnp.zeros((16, lanes), jnp.float32)
    for k in range(3):
        piece = own.astype(jnp.bfloat16).astype(jnp.float32)
        spread = jnp.where(lane == PARAMS + 16 * k + param, piece, spread)
        own = own - piece
    own_row = jnp.sum(spread, axis=0, keepdims=True)
    lane = lax.broadcasted_iota(jnp.int32, (size, lanes), 1)
    for chunk in range(CHUNKS):
        for copy in loads[chunk]:
            copy.wait()
        base = chunk * size
        rows = pl.ds(base * ROWS, size * ROWS)
        row = lambda r: pl.ds(base * ROWS + r, size, stride=ROWS)
        raw = [proj_ref[i, base : base + size].astype(jnp.float32) for i in range(3)]

        once = [pltpu.roll(x, 1, 1) for x in raw]
        twice = [pltpu.roll(x, 2, 1) for x in raw]

        def conv(i):
            tap = lambda m: columns[base : base + size, 3 * i + m : 3 * i + m + 1]
            late = tap(1) * jnp.where(lane < 1, 0.0, once[i])
            return tap(0) * raw[i] + late + tap(2) * jnp.where(lane < 2, 0.0, twice[i])

        factor_ref[base : base + size, :] = jnp.where(lane < 2, 1.0, conv(0))
        wide[row(0), :] = conv(1) * conv(2)
        for part in range(2):
            for half in range(2):
                wide[row(1 + 2 * part + half), :] = filt_ref[
                    part, base : base + size, lanes * half : lanes * (half + 1)
                ]
        fourth = pltpu.roll(raw[0], 4, 1)
        heads = jnp.where(lane < 2, raw[1], jnp.where(lane < 4, twice[2], fourth))
        tails = jnp.where(lane < 2, twice[2], jnp.where(lane < 4, fourth, raw[1]))
        edges = jnp.where(lane < 14, pltpu.roll(tails, 10, 1), own_row)
        edges = jnp.where(lane < 8, heads, edges)
        wide[row(EDGE_ROW), :] = edges
        out_ref[rows, :] = wide[rows, :].astype(jnp.bfloat16)


def channel_kernel(recv_ref, waves_ref, out_ref, gain_ref, wide):
    shards = out_ref.shape[0]
    lanes = out_ref.shape[1]
    size = 2 * shards
    wide[...] = recv_ref[...].astype(jnp.float32)
    plane = lambda r: wide[pl.ds(r, shards, stride=ROWS), :]
    lane = lax.broadcasted_iota(jnp.int32, (shards, lanes), 1)
    shard = lax.broadcasted_iota(jnp.int32, (shards, lanes), 0)
    back = lambda x, steps: pltpu.roll(x, lanes - steps, 1)
    merge = lambda x: x + back(x, 16) + back(x, 32)

    edges = plane(EDGE_ROW)
    gain_ref[...] = jnp.broadcast_to(merge(edges)[:, PARAMS + 10 : PARAMS + 11], (shards, lanes))
    me = lax.axis_index("seq")
    own = merge(wide[pl.ds(me * ROWS + EDGE_ROW, 1), :])
    param = lambda p: jnp.broadcast_to(own[:, PARAMS + p : PARAMS + p + 1], (1, lanes))
    first = lax.broadcasted_iota(jnp.int32, (1, lanes), 1)
    tap = lambda m: jnp.where(
        first < 2, param(3 + m), jnp.where(first < 4, param(6 + m), param(m))
    )
    two_ago = back(jnp.where(shard == 0, 0.0, pltpu.roll(edges, 1, 0)), 8)
    one_ago = jnp.where(lane % 2 == 1, pltpu.roll(edges, 1, 1), back(two_ago, 1))
    conv = tap(0) * edges + tap(1) * one_ago + tap(2) * two_ago
    mixed = jnp.where(lane < 2, conv * back(conv, 2), plane(0)).astype(jnp.bfloat16)

    unfold = lambda x: jnp.concatenate([x[:, :size], x[:, size:]], axis=0)
    square = lambda a, b, c, d: jnp.concatenate(
        [jnp.concatenate([a, b], axis=1), jnp.concatenate([c, d], axis=1)], axis=0
    )
    dot = lambda a, b, dims: lax.dot_general(
        a, b, (dims, ((), ())), preferred_element_type=jnp.float32
    )
    half = shards // 2
    edge = unfold(waves_ref[:half, :])
    flip = jnp.where(shard % 2 == 0, 1.0, -1.0).astype(jnp.bfloat16)
    c, d = edge[:, :shards], edge[:, shards:]
    edge = jnp.concatenate([c, c * flip, d, d * flip], axis=1)
    inner = unfold(waves_ref[half : half + lanes // 2, :])
    w_re, w_im = inner[:, :lanes], inner[:, lanes:]
    fwd, inv = square(w_re, -w_im, w_im, w_re), square(w_re, w_im, -w_im, w_re)
    turns = waves_ref[half + lanes // 2 :, :].astype(jnp.float32)
    cos, sin = turns[:, :size], turns[:, size:]

    part = dot(mixed, edge, ((0,), (0,)))
    a_re, a_im = part[:, :size], part[:, size:]
    b = jnp.concatenate([a_re * cos - a_im * sin, a_re * sin + a_im * cos], axis=0)
    spec = dot(fwd, b.astype(jnp.bfloat16), ((1,), (0,)))
    s_re, s_im = spec[:lanes], spec[lanes:]
    f_re = jnp.concatenate([plane(1), plane(2)], axis=1)
    f_im = jnp.concatenate([plane(3), plane(4)], axis=1)
    prod = jnp.concatenate([s_re * f_re - s_im * f_im, s_re * f_im + s_im * f_re], axis=0)
    time = dot(inv, prod.astype(jnp.bfloat16), ((1,), (0,)))
    c_re, c_im = time[:lanes], time[lanes:]
    d = jnp.concatenate([c_re * cos + c_im * sin, c_im * cos - c_re * sin], axis=1)
    long_out = dot(edge, d.astype(jnp.bfloat16), ((1,), (1,))) * (1.0 / (size * lanes))
    both = long_out + param(9) * mixed.astype(jnp.float32)
    out_ref[...] = jnp.where(lane < 2, back(conv, 4) * both, both)


def pack(proj, filter_spectrum, taps, skip, gain):
    chans, lanes = proj.shape[1], proj.shape[2]
    hbm = pl.BlockSpec(memory_space=pltpu.HBM)
    vmem = pl.BlockSpec(memory_space=pltpu.VMEM)
    inputs = (proj, filter_spectrum, taps, skip, gain)
    return pl.pallas_call(
        pack_kernel,
        out_shape=(
            jax.ShapeDtypeStruct((chans * ROWS, lanes), jnp.bfloat16),
            jax.ShapeDtypeStruct((chans, lanes), jnp.float32),
        ),
        in_specs=[hbm] * len(inputs),
        out_specs=(vmem, vmem),
        scratch_shapes=[
            pltpu.VMEM(proj.shape, proj.dtype),
            pltpu.VMEM(filter_spectrum.shape, filter_spectrum.dtype),
            pltpu.VMEM((16, lanes), jnp.float32),
            pltpu.VMEM((chans * ROWS, lanes), jnp.float32),
            pltpu.SemaphoreType.DMA((2, CHUNKS)),
            pltpu.SemaphoreType.DMA((5,)),
        ],
        compiler_params=pltpu.CompilerParams(vmem_limit_bytes=16 * 2**20),
    )(*(pltpu.with_memory_space_constraint(x, pltpu.HBM) for x in inputs))


def convolve(recv, waves):
    lanes = recv.shape[1]
    shards = recv.shape[0] // ROWS
    vmem = pl.BlockSpec(memory_space=pltpu.VMEM)
    return pl.pallas_call(
        channel_kernel,
        out_shape=(jax.ShapeDtypeStruct((shards, lanes), jnp.float32),) * 2,
        in_specs=[vmem] * 2,
        out_specs=(vmem,) * 2,
        scratch_shapes=[pltpu.VMEM((shards * ROWS, lanes), jnp.float32)],
        compiler_params=pltpu.CompilerParams(vmem_limit_bytes=16 * 2**20),
    )(recv, waves)


def per_device(proj, short_filter, skip_gain, norm_gain, filter_spectrum):
    chans, tok = proj.shape[1], proj.shape[2]
    peers = lax.axis_size("seq")
    groups = lax.axis_size("tp")
    waves = tables(peers, tok)
    taps = jnp.swapaxes(short_filter, 1, 2)
    sent, factor = pack(proj, filter_spectrum, taps, skip_gain[None], norm_gain[None])
    recv = lax.all_to_all(
        sent.reshape(peers, ROWS // 2, 2, tok), "seq", split_axis=0, concat_axis=0, tiled=True
    )
    part, gain = convolve(recv.reshape(peers * ROWS, tok), waves)
    part = lax.all_to_all(
        part.reshape(peers, 1, tok), "seq", split_axis=0, concat_axis=0, tiled=True
    )
    pre = part.reshape(chans, tok) * factor
    squares = jnp.broadcast_to(jnp.sum(pre * pre, axis=0)[None, None], (groups, 1, tok))
    squares = lax.all_to_all(squares, "tp", split_axis=0, concat_axis=0, tiled=True)
    meansq = jnp.sum(squares[:, 0], axis=0) / (chans * groups)
    return (pre * lax.rsqrt(meansq + 1e-05)[None, :] * gain).astype(jnp.bfloat16)


def solution(mesh):
    return jax.shard_map(
        per_device,
        mesh=mesh,
        in_specs=(
            P(None, "tp", "seq"),
            P(None, "tp", None),
            P("tp"),
            P("tp"),
            P(None, "tp", "seq"),
        ),
        out_specs=P("tp", "seq"),
        check_vma=False,
    )
```

```python
import jax
import jax.numpy as jnp
import numpy as np
from jax import lax
from jax.experimental import pallas as pl
from jax.experimental.pallas import tpu as pltpu
from jax.sharding import PartitionSpec as P

ROWS = 6
EDGE_ROW = 5
CHUNKS = 1


def tables(n_coarse, n_fine):
    total = 2 * n_coarse * n_fine
    n1 = np.arange(n_coarse)
    k1 = np.arange(2 * n_coarse)
    n2 = np.arange(n_fine)
    turn = 2.0 * np.pi * (np.outer(n2, k1) % total) / total
    first = 2.0 * np.pi * (np.outer(n1, k1[:n_coarse]) % (2 * n_coarse)) / (2 * n_coarse)
    edge = np.concatenate([np.cos(first), -np.sin(first)], axis=1)
    inner = 2.0 * np.pi * (np.outer(n2, n2) % n_fine) / n_fine
    inner = np.concatenate([np.cos(inner), -np.sin(inner)], axis=1)
    fold = lambda x: np.concatenate([x[: len(x) // 2], x[len(x) // 2 :]], axis=1)
    turns = np.concatenate([np.cos(turn), -np.sin(turn)], axis=1)
    rows = [fold(edge), fold(inner), turns]
    return jnp.asarray(np.concatenate(rows, axis=0), jnp.bfloat16)


def pack_kernel(
    proj_hbm, filt_hbm, taps_hbm, skip_hbm, gain_hbm,
    out_ref, query_ref, columns_ref, own_ref,
    proj_ref, filt_ref, taps_ref, small_ref, wide, sem_in, sem_small
):
    chans = proj_ref.shape[1]
    lanes = proj_ref.shape[2]
    size = chans // CHUNKS
    small = [
        pltpu.make_async_copy(taps_hbm, taps_ref, sem_small.at[0]),
        pltpu.make_async_copy(skip_hbm, small_ref.at[pl.ds(9, 1)], sem_small.at[1]),
        pltpu.make_async_copy(gain_hbm, small_ref.at[pl.ds(10, 1)], sem_small.at[2]),
    ]
    loads = []
    for chunk in range(CHUNKS):
        part = pl.ds(chunk * size, size)
        loads.append([
            pltpu.make_async_copy(proj_hbm.at[:, part], proj_ref.at[:, part], sem_in.at[0, chunk]),
            pltpu.make_async_copy(filt_hbm.at[:, part], filt_ref.at[:, part], sem_in.at[1, chunk]),
        ])
    for copy in small + sum(loads, []):
        copy.start()
    for copy in small:
        copy.wait()
    for i in range(3):
        small_ref[3 * i : 3 * i + 3, :] = taps_ref[i]
    lane = lax.broadcasted_iota(jnp.int32, (16, lanes), 1)
    param = lax.broadcasted_iota(jnp.int32, (16, lanes), 0)
    params = jnp.where(param < 11, small_ref[...], 0.0)
    columns = params.T
    columns_ref[...] = columns
    mine = jnp.where(lane == lax.axis_index("seq"), params, 0.0)
    own_ref[...] = jnp.broadcast_to(jnp.sum(mine, axis=1, keepdims=True), (16, lanes))
    lane = lax.broadcasted_iota(jnp.int32, (size, lanes), 1)
    for chunk in range(CHUNKS):
        for copy in loads[chunk]:
            copy.wait()
        base = chunk * size
        rows = pl.ds(base * ROWS, size * ROWS)
        row = lambda r: pl.ds(base * ROWS + r, size, stride=ROWS)
        raw = [proj_ref[i, base : base + size].astype(jnp.float32) for i in range(3)]

        twice = [None] + [pltpu.roll(x, 2, 1) for x in raw[1:]]

        def conv(i):
            tap = lambda m: columns[base : base + size, 3 * i + m : 3 * i + m + 1]
            late = tap(1) * jnp.where(lane < 1, 0.0, pltpu.roll(raw[i], 1, 1))
            return tap(0) * raw[i] + late + tap(2) * jnp.where(lane < 2, 0.0, twice[i])

        query_ref[base : base + size, :] = proj_ref[0, base : base + size]
        wide[row(0), :] = conv(1) * conv(2)
        for part in range(2):
            for half in range(2):
                wide[row(1 + 2 * part + half), :] = filt_ref[
                    part, base : base + size, lanes * half : lanes * (half + 1)
                ]
        fourth = pltpu.roll(raw[0], 4, 1)
        heads = jnp.where(lane < 2, raw[1], jnp.where(lane < 4, twice[2], fourth))
        tails = jnp.where(lane < 2, twice[2], jnp.where(lane < 4, fourth, raw[1]))
        edges = jnp.where(lane < 8, heads, pltpu.roll(tails, 10, 1))
        wide[row(EDGE_ROW), :] = edges
        out_ref[rows, :] = wide[rows, :].astype(jnp.bfloat16)


def channel_kernel(
    recv_ref, query_ref, columns_ref, own_ref, waves_ref, out_ref, factor_ref, gain_ref, wide
):
    shards = out_ref.shape[0]
    lanes = out_ref.shape[1]
    size = 2 * shards
    wide[...] = recv_ref[...].astype(jnp.float32)
    plane = lambda r: wide[pl.ds(r, shards, stride=ROWS), :]
    lane = lax.broadcasted_iota(jnp.int32, (shards, lanes), 1)
    shard = lax.broadcasted_iota(jnp.int32, (shards, lanes), 0)

    edges = plane(EDGE_ROW).T
    at = lax.broadcasted_iota(jnp.int32, (8, shards), 0)
    column = lax.broadcasted_iota(jnp.int32, (8, shards), 1)
    own = lambda p: own_ref[p : p + 1, :]
    tap = lambda m: jnp.where(at < 2, own(3 + m), jnp.where(at < 4, own(6 + m), own(m)))
    heads = edges[:8]
    two_ago = jnp.where(column == 0, 0.0, pltpu.roll(edges[8:16], 1, 1))
    one_ago = jnp.where(at % 2 == 1, pltpu.roll(heads, 1, 0), pltpu.roll(two_ago, 7, 0))
    conv = tap(0) * heads + tap(1) * one_ago + tap(2) * two_ago
    repair = (conv * pltpu.roll(conv, 6, 0)).astype(jnp.bfloat16).astype(jnp.float32)
    upright = plane(0).T
    mixed = jnp.concatenate([jnp.where(at < 2, repair, upright[:8]), upright[8:]], axis=0)
    rest = jnp.zeros((lanes - 8, shards), jnp.float32)
    spread = lambda x: jnp.concatenate([x, rest], axis=0).T
    skipped = own(9) * jnp.where(lane < 2, spread(repair), plane(0))
    query = spread(pltpu.roll(conv, 4, 0))

    unfold = lambda x: jnp.concatenate([x[:, :size], x[:, size:]], axis=0)
    square = lambda a, b, c, d: jnp.concatenate(
        [jnp.concatenate([a, b], axis=1), jnp.concatenate([c, d], axis=1)], axis=0
    )
    dot = lambda a, b, dims: lax.dot_general(
        a, b, (dims, ((), ())), preferred_element_type=jnp.float32
    )
    half = shards // 2
    edge = unfold(waves_ref[:half, :])
    flip = jnp.where(shard % 2 == 0, 1.0, -1.0).astype(jnp.bfloat16)
    c, d = edge[:, :shards], edge[:, shards:]
    edge = jnp.concatenate([c, c * flip, d, d * flip], axis=1)
    inner = unfold(waves_ref[half : half + lanes // 2, :])
    w_re, w_im = inner[:, :lanes], inner[:, lanes:]
    fwd, inv = square(w_re, -w_im, w_im, w_re), square(w_re, w_im, -w_im, w_re)
    turns = waves_ref[half + lanes // 2 :, :].astype(jnp.float32)
    cos, sin = turns[:, :size], turns[:, size:]

    part = dot(mixed.astype(jnp.bfloat16), edge, ((1,), (0,)))
    a_re, a_im = part[:, :size], part[:, size:]
    b = jnp.concatenate([a_re * cos - a_im * sin, a_re * sin + a_im * cos], axis=0)
    spec = dot(fwd, b.astype(jnp.bfloat16), ((1,), (0,)))
    s_re, s_im = spec[:lanes], spec[lanes:]
    f_re = jnp.concatenate([plane(1), plane(2)], axis=1)
    f_im = jnp.concatenate([plane(3), plane(4)], axis=1)
    prod = jnp.concatenate([s_re * f_re - s_im * f_im, s_re * f_im + s_im * f_re], axis=0)
    time = dot(inv, prod.astype(jnp.bfloat16), ((1,), (0,)))
    c_re, c_im = time[:lanes], time[lanes:]
    d = jnp.concatenate([c_re * cos + c_im * sin, c_im * cos - c_re * sin], axis=1)
    long_out = dot(edge, d.astype(jnp.bfloat16), ((1,), (1,))) * (1.0 / (size * lanes))
    raw = query_ref[...].astype(jnp.float32)
    weight = lambda p: columns_ref[:, p : p + 1]
    gain_ref[...] = jnp.broadcast_to(weight(10), (shards, lanes))
    late = weight(1) * jnp.where(lane < 1, 0.0, pltpu.roll(raw, 1, 1))
    late = weight(0) * raw + late + weight(2) * jnp.where(lane < 2, 0.0, pltpu.roll(raw, 2, 1))
    factor_ref[...] = jnp.where(lane < 2, 1.0, late)
    both = long_out + skipped
    out_ref[...] = jnp.where(lane < 2, query * both, both)


def pack(proj, filter_spectrum, taps, skip, gain):
    chans, lanes = proj.shape[1], proj.shape[2]
    hbm = pl.BlockSpec(memory_space=pltpu.HBM)
    vmem = pl.BlockSpec(memory_space=pltpu.VMEM)
    inputs = (proj, filter_spectrum, taps, skip, gain)
    return pl.pallas_call(
        pack_kernel,
        out_shape=(
            jax.ShapeDtypeStruct((chans * ROWS, lanes), jnp.bfloat16),
            jax.ShapeDtypeStruct((chans, lanes), jnp.bfloat16),
            jax.ShapeDtypeStruct((chans, 16), jnp.float32),
            jax.ShapeDtypeStruct((16, lanes), jnp.float32),
        ),
        in_specs=[hbm] * len(inputs),
        out_specs=(vmem,) * 4,
        scratch_shapes=[
            pltpu.VMEM(proj.shape, proj.dtype),
            pltpu.VMEM(filter_spectrum.shape, filter_spectrum.dtype),
            pltpu.VMEM(taps.shape, taps.dtype),
            pltpu.VMEM((16, lanes), jnp.float32),
            pltpu.VMEM((chans * ROWS, lanes), jnp.float32),
            pltpu.SemaphoreType.DMA((2, CHUNKS)),
            pltpu.SemaphoreType.DMA((3,)),
        ],
        compiler_params=pltpu.CompilerParams(vmem_limit_bytes=16 * 2**20),
    )(*(pltpu.with_memory_space_constraint(x, pltpu.HBM) for x in inputs))


def convolve(recv, query, columns, own, waves):
    lanes = recv.shape[1]
    shards = recv.shape[0] // ROWS
    vmem = pl.BlockSpec(memory_space=pltpu.VMEM)
    return pl.pallas_call(
        channel_kernel,
        out_shape=(jax.ShapeDtypeStruct((shards, lanes), jnp.float32),) * 3,
        in_specs=[vmem] * 5,
        out_specs=(vmem,) * 3,
        scratch_shapes=[pltpu.VMEM((shards * ROWS, lanes), jnp.float32)],
        compiler_params=pltpu.CompilerParams(vmem_limit_bytes=16 * 2**20),
    )(recv, query, columns, own, waves)


def per_device(proj, short_filter, skip_gain, norm_gain, filter_spectrum):
    chans, tok = proj.shape[1], proj.shape[2]
    peers = lax.axis_size("seq")
    groups = lax.axis_size("tp")
    waves = tables(peers, tok)
    taps = jnp.swapaxes(short_filter, 1, 2)
    sent, query, columns, own = pack(proj, filter_spectrum, taps, skip_gain[None], norm_gain[None])
    recv = lax.all_to_all(
        sent.reshape(peers, ROWS // 2, 2, tok), "seq", split_axis=0, concat_axis=0, tiled=True
    )
    recv = recv.reshape(peers * ROWS, tok)
    part, factor, gain = convolve(recv, query, columns, own, waves)
    part = lax.all_to_all(
        part.reshape(peers, 1, tok), "seq", split_axis=0, concat_axis=0, tiled=True
    )
    pre = part.reshape(chans, tok) * factor
    squares = lax.all_gather(jnp.sum(pre * pre, axis=0)[None], "tp", axis=0, tiled=True)
    meansq = jnp.sum(squares, axis=0) / (chans * groups)
    return (pre * lax.rsqrt(meansq + 1e-05)[None, :] * gain).astype(jnp.bfloat16)


def solution(mesh):
    return jax.shard_map(
        per_device,
        mesh=mesh,
        in_specs=(
            P(None, "tp", "seq"),
            P(None, "tp", None),
            P("tp"),
            P("tp"),
            P(None, "tp", "seq"),
        ),
        out_specs=P("tp", "seq"),
        check_vma=False,
    )
```

```python
import jax
import jax.numpy as jnp
import numpy as np
from jax import lax
from jax.experimental import pallas as pl
from jax.experimental.pallas import tpu as pltpu
from jax.sharding import PartitionSpec as P

ROWS = 6
EDGE_ROW = 5


def tables(n_coarse, n_fine):
    total = 2 * n_coarse * n_fine
    n1 = np.arange(n_coarse)
    k1 = np.arange(2 * n_coarse)
    n2 = np.arange(n_fine)
    turn = 2.0 * np.pi * (np.outer(n2, k1) % total) / total
    first = 2.0 * np.pi * (np.outer(n1, k1[:n_coarse]) % (2 * n_coarse)) / (2 * n_coarse)
    edge = np.concatenate([np.cos(first), -np.sin(first)], axis=1)
    inner = 2.0 * np.pi * (np.outer(n2, n2) % n_fine) / n_fine
    inner = np.concatenate([np.cos(inner), -np.sin(inner)], axis=1)
    fold = lambda x: np.concatenate([x[: len(x) // 2], x[len(x) // 2 :]], axis=1)
    turns = np.concatenate([np.cos(turn), -np.sin(turn)], axis=1)
    rows = [fold(edge), fold(inner), turns]
    return jnp.asarray(np.concatenate(rows, axis=0), jnp.bfloat16)


def pack_kernel(
    proj_hbm, filt_hbm, taps_hbm, skip_hbm, gain_hbm,
    out_ref, query_ref, columns_ref, own_ref,
    proj_ref, filt_ref, taps_ref, small_ref, wide, sem_in, sem_small
):
    chans = proj_ref.shape[1]
    lanes = proj_ref.shape[2]
    small = [
        pltpu.make_async_copy(taps_hbm, taps_ref, sem_small.at[0]),
        pltpu.make_async_copy(skip_hbm, small_ref.at[pl.ds(9, 1)], sem_small.at[1]),
        pltpu.make_async_copy(gain_hbm, small_ref.at[pl.ds(10, 1)], sem_small.at[2]),
    ]
    proj_loads = [
        pltpu.make_async_copy(proj_hbm.at[:], proj_ref.at[:], sem_in.at[0, k])
        for k in range(1)
    ]
    filt_loads = [
        pltpu.make_async_copy(filt_hbm.at[k], filt_ref.at[k], sem_in.at[1, k])
        for k in range(2)
    ]
    for copy in small + proj_loads + filt_loads:
        copy.start()
    for copy in small:
        copy.wait()
    for i in range(3):
        small_ref[3 * i : 3 * i + 3, :] = taps_ref[i]
    lane = lax.broadcasted_iota(jnp.int32, (16, lanes), 1)
    param = lax.broadcasted_iota(jnp.int32, (16, lanes), 0)
    params = jnp.where(param < 11, small_ref[...], 0.0)
    columns = params.T
    columns_ref[...] = columns
    mine = jnp.where(lane == lax.axis_index("seq"), params, 0.0)
    own_ref[...] = jnp.broadcast_to(jnp.sum(mine, axis=1, keepdims=True), (16, lanes))
    lane = lax.broadcasted_iota(jnp.int32, (chans, lanes), 1)
    row = lambda r: pl.ds(r, chans, stride=ROWS)
    for copy in proj_loads:
        copy.wait()
    raw = [proj_ref[i].astype(jnp.float32) for i in range(3)]
    twice = [None] + [pltpu.roll(x, 2, 1) for x in raw[1:]]

    def conv(i):
        tap = lambda m: columns[:, 3 * i + m : 3 * i + m + 1]
        late = tap(1) * jnp.where(lane < 1, 0.0, pltpu.roll(raw[i], 1, 1))
        return tap(0) * raw[i] + late + tap(2) * jnp.where(lane < 2, 0.0, twice[i])

    query_ref[...] = proj_ref[0]
    wide[row(0), :] = conv(1) * conv(2)
    fourth = pltpu.roll(raw[0], 4, 1)
    heads = jnp.where(lane < 2, raw[1], jnp.where(lane < 4, twice[2], fourth))
    tails = jnp.where(lane < 2, twice[2], jnp.where(lane < 4, fourth, raw[1]))
    wide[row(EDGE_ROW), :] = jnp.where(lane < 8, heads, pltpu.roll(tails, 10, 1))
    for copy in filt_loads:
        copy.wait()
    for part in range(2):
        for half in range(2):
            wide[row(1 + 2 * part + half), :] = filt_ref[
                part, :, lanes * half : lanes * (half + 1)
            ]
    out_ref[...] = wide[...].astype(jnp.bfloat16)


def channel_kernel(
    recv_ref, query_ref, columns_ref, own_ref, waves_ref, out_ref, factor_ref, gain_ref, wide
):
    shards = out_ref.shape[0]
    lanes = out_ref.shape[1]
    size = 2 * shards
    wide[...] = recv_ref[...].astype(jnp.float32)
    plane = lambda r: wide[pl.ds(r, shards, stride=ROWS), :]
    lane = lax.broadcasted_iota(jnp.int32, (shards, lanes), 1)
    shard = lax.broadcasted_iota(jnp.int32, (shards, lanes), 0)

    edges = plane(EDGE_ROW).T
    at = lax.broadcasted_iota(jnp.int32, (8, shards), 0)
    column = lax.broadcasted_iota(jnp.int32, (8, shards), 1)
    own = lambda p: own_ref[p : p + 1, :]
    tap = lambda m: jnp.where(at < 2, own(3 + m), jnp.where(at < 4, own(6 + m), own(m)))
    heads = edges[:8]
    two_ago = jnp.where(column == 0, 0.0, pltpu.roll(edges[8:16], 1, 1))
    one_ago = jnp.where(at % 2 == 1, pltpu.roll(heads, 1, 0), pltpu.roll(two_ago, 7, 0))
    conv = tap(0) * heads + tap(1) * one_ago + tap(2) * two_ago
    repair = (conv * pltpu.roll(conv, 6, 0)).astype(jnp.bfloat16).astype(jnp.float32)
    upright = plane(0).T
    mixed = jnp.concatenate([jnp.where(at < 2, repair, upright[:8]), upright[8:]], axis=0)
    rest = jnp.zeros((lanes - 8, shards), jnp.float32)
    spread = lambda x: jnp.concatenate([x, rest], axis=0).T
    skipped = own(9) * jnp.where(lane < 2, spread(repair), plane(0))
    query = spread(pltpu.roll(conv, 4, 0))

    unfold = lambda x: jnp.concatenate([x[:, :size], x[:, size:]], axis=0)
    square = lambda a, b, c, d: jnp.concatenate(
        [jnp.concatenate([a, b], axis=1), jnp.concatenate([c, d], axis=1)], axis=0
    )
    dot = lambda a, b, dims: lax.dot_general(
        a, b, (dims, ((), ())), preferred_element_type=jnp.float32
    )
    half = shards // 2
    edge = unfold(waves_ref[:half, :])
    flip = jnp.where(shard % 2 == 0, 1.0, -1.0).astype(jnp.bfloat16)
    c, d = edge[:, :shards], edge[:, shards:]
    edge = jnp.concatenate([c, c * flip, d, d * flip], axis=1)
    inner = unfold(waves_ref[half : half + lanes // 2, :])
    w_re, w_im = inner[:, :lanes], inner[:, lanes:]
    fwd, inv = square(w_re, -w_im, w_im, w_re), square(w_re, w_im, -w_im, w_re)
    turns = waves_ref[half + lanes // 2 :, :].astype(jnp.float32)
    cos, sin = turns[:, :size], turns[:, size:]

    part = dot(mixed.astype(jnp.bfloat16), edge, ((1,), (0,)))
    a_re, a_im = part[:, :size], part[:, size:]
    b = jnp.concatenate([a_re * cos - a_im * sin, a_re * sin + a_im * cos], axis=0)
    spec = dot(fwd, b.astype(jnp.bfloat16), ((1,), (0,)))
    s_re, s_im = spec[:lanes], spec[lanes:]
    f_re = jnp.concatenate([plane(1), plane(2)], axis=1)
    f_im = jnp.concatenate([plane(3), plane(4)], axis=1)
    prod = jnp.concatenate([s_re * f_re - s_im * f_im, s_re * f_im + s_im * f_re], axis=0)
    time = dot(inv, prod.astype(jnp.bfloat16), ((1,), (0,)))
    c_re, c_im = time[:lanes], time[lanes:]
    d = jnp.concatenate([c_re * cos + c_im * sin, c_im * cos - c_re * sin], axis=1)
    long_out = dot(edge, d.astype(jnp.bfloat16), ((1,), (1,))) * (1.0 / (size * lanes))
    raw = query_ref[...].astype(jnp.float32)
    weight = lambda p: columns_ref[:, p : p + 1]
    gain_ref[...] = jnp.broadcast_to(weight(10), (shards, lanes))
    late = weight(1) * jnp.where(lane < 1, 0.0, pltpu.roll(raw, 1, 1))
    late = weight(0) * raw + late + weight(2) * jnp.where(lane < 2, 0.0, pltpu.roll(raw, 2, 1))
    factor_ref[...] = jnp.where(lane < 2, 1.0, late)
    both = long_out + skipped
    out_ref[...] = jnp.where(lane < 2, query * both, both)


def pack(proj, filter_spectrum, taps, skip, gain):
    chans, lanes = proj.shape[1], proj.shape[2]
    hbm = pl.BlockSpec(memory_space=pltpu.HBM)
    vmem = pl.BlockSpec(memory_space=pltpu.VMEM)
    inputs = (proj, filter_spectrum, taps, skip, gain)
    return pl.pallas_call(
        pack_kernel,
        out_shape=(
            jax.ShapeDtypeStruct((chans * ROWS, lanes), jnp.bfloat16),
            jax.ShapeDtypeStruct((chans, lanes), jnp.bfloat16),
            jax.ShapeDtypeStruct((chans, 16), jnp.float32),
            jax.ShapeDtypeStruct((16, lanes), jnp.float32),
        ),
        in_specs=[hbm] * len(inputs),
        out_specs=(vmem,) * 4,
        scratch_shapes=[
            pltpu.VMEM(proj.shape, proj.dtype),
            pltpu.VMEM(filter_spectrum.shape, filter_spectrum.dtype),
            pltpu.VMEM(taps.shape, taps.dtype),
            pltpu.VMEM((16, lanes), jnp.float32),
            pltpu.VMEM((chans * ROWS, lanes), jnp.float32),
            pltpu.SemaphoreType.DMA((2, 4)),
            pltpu.SemaphoreType.DMA((3,)),
        ],
        compiler_params=pltpu.CompilerParams(vmem_limit_bytes=16 * 2**20),
    )(*(pltpu.with_memory_space_constraint(x, pltpu.HBM) for x in inputs))


def convolve(recv, query, columns, own, waves):
    lanes = recv.shape[1]
    shards = recv.shape[0] // ROWS
    vmem = pl.BlockSpec(memory_space=pltpu.VMEM)
    return pl.pallas_call(
        channel_kernel,
        out_shape=(jax.ShapeDtypeStruct((shards, lanes), jnp.float32),) * 3,
        in_specs=[vmem] * 5,
        out_specs=(vmem,) * 3,
        scratch_shapes=[pltpu.VMEM((shards * ROWS, lanes), jnp.float32)],
        compiler_params=pltpu.CompilerParams(vmem_limit_bytes=16 * 2**20),
    )(recv, query, columns, own, waves)


def per_device(proj, short_filter, skip_gain, norm_gain, filter_spectrum):
    chans, tok = proj.shape[1], proj.shape[2]
    peers = lax.axis_size("seq")
    groups = lax.axis_size("tp")
    waves = tables(peers, tok)
    taps = jnp.swapaxes(short_filter, 1, 2)
    sent, query, columns, own = pack(proj, filter_spectrum, taps, skip_gain[None], norm_gain[None])
    recv = lax.all_to_all(
        sent.reshape(peers, ROWS // 2, 2, tok), "seq", split_axis=0, concat_axis=0, tiled=True
    )
    recv = recv.reshape(peers * ROWS, tok)
    part, factor, gain = convolve(recv, query, columns, own, waves)
    part = lax.all_to_all(
        part.reshape(peers, 1, tok), "seq", split_axis=0, concat_axis=0, tiled=True
    )
    pre = part.reshape(chans, tok) * factor
    squares = lax.all_gather(jnp.sum(pre * pre, axis=0)[None], "tp", axis=0, tiled=True)
    meansq = jnp.sum(squares, axis=0) / (chans * groups)
    return (pre * lax.rsqrt(meansq + 1e-05)[None, :] * gain).astype(jnp.bfloat16)


def solution(mesh):
    return jax.shard_map(
        per_device,
        mesh=mesh,
        in_specs=(
            P(None, "tp", "seq"),
            P(None, "tp", None),
            P("tp"),
            P("tp"),
            P(None, "tp", "seq"),
        ),
        out_specs=P("tp", "seq"),
        check_vma=False,
    )
```

```python
import jax
import jax.numpy as jnp
import numpy as np
from jax import lax
from jax.experimental import pallas as pl
from jax.experimental.pallas import tpu as pltpu
from jax.sharding import PartitionSpec as P

ROWS = 6
EDGE_ROW = 5
SPARE = 16


def tables(n_coarse, n_fine):
    total = 2 * n_coarse * n_fine
    n1 = np.arange(n_coarse)
    k1 = np.arange(2 * n_coarse)
    n2 = np.arange(n_fine)
    turn = 2.0 * np.pi * (np.outer(n2, k1) % total) / total
    first = 2.0 * np.pi * (np.outer(n1, k1[:n_coarse]) % (2 * n_coarse)) / (2 * n_coarse)
    edge = np.concatenate([np.cos(first), -np.sin(first)], axis=1)
    inner = 2.0 * np.pi * (np.outer(n2, n2) % n_fine) / n_fine
    inner = np.concatenate([np.cos(inner), -np.sin(inner)], axis=1)
    fold = lambda x: np.concatenate([x[: len(x) // 2], x[len(x) // 2 :]], axis=1)
    turns = np.concatenate([np.cos(turn), -np.sin(turn)], axis=1)
    rows = [fold(edge), fold(inner), turns]
    return jnp.asarray(np.concatenate(rows, axis=0), jnp.bfloat16)


def pack_kernel(
    proj_hbm, filt_hbm, taps_hbm, skip_hbm, gain_hbm,
    out_ref, query_ref, columns_ref, own_ref,
    proj_ref, filt_ref, taps_ref, small_ref, wide, sem_in, sem_small
):
    chans = proj_ref.shape[1]
    lanes = proj_ref.shape[2]
    small = [
        pltpu.make_async_copy(taps_hbm, taps_ref.at[pl.ds(0, 3)], sem_small.at[0]),
        pltpu.make_async_copy(skip_hbm, small_ref.at[pl.ds(9, 1)], sem_small.at[1]),
        pltpu.make_async_copy(gain_hbm, small_ref.at[pl.ds(10, 1)], sem_small.at[2]),
    ]
    proj_loads = [
        pltpu.make_async_copy(proj_hbm.at[:], proj_ref.at[:], sem_in.at[0, k])
        for k in range(1)
    ]
    filt_loads = [
        pltpu.make_async_copy(filt_hbm.at[k], filt_ref.at[k], sem_in.at[1, k])
        for k in range(2)
    ]
    for copy in small + proj_loads + filt_loads:
        copy.start()
    for copy in small:
        copy.wait()
    for i in range(3):
        small_ref[3 * i : 3 * i + 3, :] = taps_ref[i]
    lane = lax.broadcasted_iota(jnp.int32, (16, lanes), 1)
    param = lax.broadcasted_iota(jnp.int32, (16, lanes), 0)
    params = jnp.where(param < 11, small_ref[...], 0.0)
    columns = params.T
    columns_ref[...] = columns
    mine = jnp.where(lane == lax.axis_index("seq"), params, 0.0)
    own_ref[...] = jnp.broadcast_to(jnp.sum(mine, axis=1, keepdims=True), (16, lanes))
    lane = lax.broadcasted_iota(jnp.int32, (chans, lanes), 1)
    row = lambda r: pl.ds(r, chans, stride=ROWS)
    for copy in proj_loads:
        copy.wait()
    raw = [proj_ref[i].astype(jnp.float32) for i in range(3)]
    twice = [None] + [pltpu.roll(x, 2, 1) for x in raw[1:]]

    def conv(i):
        tap = lambda m: columns[:, 3 * i + m : 3 * i + m + 1]
        late = tap(1) * jnp.where(lane < 1, 0.0, pltpu.roll(raw[i], 1, 1))
        return tap(0) * raw[i] + late + tap(2) * jnp.where(lane < 2, 0.0, twice[i])

    query_ref[...] = proj_ref[0]
    wide[row(0), :] = conv(1) * conv(2)
    fourth = pltpu.roll(raw[0], 4, 1)
    heads = jnp.where(lane < 2, raw[1], jnp.where(lane < 4, twice[2], fourth))
    tails = jnp.where(lane < 2, twice[2], jnp.where(lane < 4, fourth, raw[1]))
    wide[row(EDGE_ROW), :] = jnp.where(lane < 8, heads, pltpu.roll(tails, 10, 1))
    for copy in filt_loads:
        copy.wait()
    for part in range(2):
        for half in range(2):
            wide[row(1 + 2 * part + half), :] = filt_ref[
                part, :, lanes * half : lanes * (half + 1)
            ]
    out_ref[...] = wide[: chans * ROWS, :].astype(jnp.bfloat16)


def channel_kernel(
    recv_ref, query_ref, columns_ref, own_ref, waves_ref, out_ref, factor_ref, gain_ref, wide
):
    shards = out_ref.shape[0]
    lanes = out_ref.shape[1]
    size = 2 * shards
    wide[: shards * ROWS, :] = recv_ref[...].astype(jnp.float32)
    plane = lambda r: wide[pl.ds(r, shards, stride=ROWS), :]
    lane = lax.broadcasted_iota(jnp.int32, (shards, lanes), 1)
    shard = lax.broadcasted_iota(jnp.int32, (shards, lanes), 0)

    edges = plane(EDGE_ROW).T
    at = lax.broadcasted_iota(jnp.int32, (8, shards), 0)
    column = lax.broadcasted_iota(jnp.int32, (8, shards), 1)
    own = lambda p: own_ref[p : p + 1, :]
    tap = lambda m: jnp.where(at < 2, own(3 + m), jnp.where(at < 4, own(6 + m), own(m)))
    heads = edges[:8]
    two_ago = jnp.where(column == 0, 0.0, pltpu.roll(edges[8:16], 1, 1))
    one_ago = jnp.where(at % 2 == 1, pltpu.roll(heads, 1, 0), pltpu.roll(two_ago, 7, 0))
    conv = tap(0) * heads + tap(1) * one_ago + tap(2) * two_ago
    repair = (conv * pltpu.roll(conv, 6, 0)).astype(jnp.bfloat16).astype(jnp.float32)
    upright = plane(0).T
    mixed = jnp.concatenate([jnp.where(at < 2, repair, upright[:8]), upright[8:]], axis=0)
    rest = jnp.zeros((lanes - 8, shards), jnp.float32)
    spread = lambda x: jnp.concatenate([x, rest], axis=0).T
    skipped = own(9) * jnp.where(lane < 2, spread(repair), plane(0))
    query = spread(pltpu.roll(conv, 4, 0))

    unfold = lambda x: jnp.concatenate([x[:, :size], x[:, size:]], axis=0)
    square = lambda a, b, c, d: jnp.concatenate(
        [jnp.concatenate([a, b], axis=1), jnp.concatenate([c, d], axis=1)], axis=0
    )
    dot = lambda a, b, dims: lax.dot_general(
        a, b, (dims, ((), ())), preferred_element_type=jnp.float32
    )
    half = shards // 2
    edge = unfold(waves_ref[:half, :])
    flip = jnp.where(shard % 2 == 0, 1.0, -1.0).astype(jnp.bfloat16)
    c, d = edge[:, :shards], edge[:, shards:]
    edge = jnp.concatenate([c, c * flip, d, d * flip], axis=1)
    inner = unfold(waves_ref[half : half + lanes // 2, :])
    w_re, w_im = inner[:, :lanes], inner[:, lanes:]
    fwd, inv = square(w_re, -w_im, w_im, w_re), square(w_re, w_im, -w_im, w_re)
    turns = waves_ref[half + lanes // 2 :, :].astype(jnp.float32)
    cos, sin = turns[:, :size], turns[:, size:]

    part = dot(mixed.astype(jnp.bfloat16), edge, ((1,), (0,)))
    a_re, a_im = part[:, :size], part[:, size:]
    b = jnp.concatenate([a_re * cos - a_im * sin, a_re * sin + a_im * cos], axis=0)
    spec = dot(fwd, b.astype(jnp.bfloat16), ((1,), (0,)))
    s_re, s_im = spec[:lanes], spec[lanes:]
    f_re = jnp.concatenate([plane(1), plane(2)], axis=1)
    f_im = jnp.concatenate([plane(3), plane(4)], axis=1)
    prod = jnp.concatenate([s_re * f_re - s_im * f_im, s_re * f_im + s_im * f_re], axis=0)
    time = dot(inv, prod.astype(jnp.bfloat16), ((1,), (0,)))
    c_re, c_im = time[:lanes], time[lanes:]
    d = jnp.concatenate([c_re * cos + c_im * sin, c_im * cos - c_re * sin], axis=1)
    long_out = dot(edge, d.astype(jnp.bfloat16), ((1,), (1,))) * (1.0 / (size * lanes))
    raw = query_ref[...].astype(jnp.float32)
    weight = lambda p: columns_ref[:, p : p + 1]
    gain_ref[...] = jnp.broadcast_to(weight(10), (shards, lanes))
    late = weight(1) * jnp.where(lane < 1, 0.0, pltpu.roll(raw, 1, 1))
    late = weight(0) * raw + late + weight(2) * jnp.where(lane < 2, 0.0, pltpu.roll(raw, 2, 1))
    factor_ref[...] = jnp.where(lane < 2, 1.0, late)
    both = long_out + skipped
    out_ref[...] = jnp.where(lane < 2, query * both, both)


def pack(proj, filter_spectrum, taps, skip, gain):
    chans, lanes = proj.shape[1], proj.shape[2]
    hbm = pl.BlockSpec(memory_space=pltpu.HBM)
    vmem = pl.BlockSpec(memory_space=pltpu.VMEM)
    inputs = (proj, filter_spectrum, taps, skip, gain)
    return pl.pallas_call(
        pack_kernel,
        out_shape=(
            jax.ShapeDtypeStruct((chans * ROWS, lanes), jnp.bfloat16),
            jax.ShapeDtypeStruct((chans, lanes), jnp.bfloat16),
            jax.ShapeDtypeStruct((chans, 16), jnp.float32),
            jax.ShapeDtypeStruct((16, lanes), jnp.float32),
        ),
        in_specs=[hbm] * len(inputs),
        out_specs=(vmem,) * 4,
        scratch_shapes=[
            pltpu.VMEM(proj.shape, proj.dtype),
            pltpu.VMEM(filter_spectrum.shape, filter_spectrum.dtype),
            pltpu.VMEM((6,) + taps.shape[1:], taps.dtype),
            pltpu.VMEM((16, lanes), jnp.float32),
            pltpu.VMEM((chans * ROWS + SPARE, lanes), jnp.float32),
            pltpu.SemaphoreType.DMA((2, 4)),
            pltpu.SemaphoreType.DMA((3,)),
        ],
        compiler_params=pltpu.CompilerParams(vmem_limit_bytes=16 * 2**20),
    )(*(pltpu.with_memory_space_constraint(x, pltpu.HBM) for x in inputs))


def convolve(recv, query, columns, own, waves):
    lanes = recv.shape[1]
    shards = recv.shape[0] // ROWS
    vmem = pl.BlockSpec(memory_space=pltpu.VMEM)
    return pl.pallas_call(
        channel_kernel,
        out_shape=(jax.ShapeDtypeStruct((shards, lanes), jnp.float32),) * 3,
        in_specs=[vmem] * 5,
        out_specs=(vmem,) * 3,
        scratch_shapes=[pltpu.VMEM((shards * ROWS + SPARE, lanes), jnp.float32)],
        compiler_params=pltpu.CompilerParams(vmem_limit_bytes=16 * 2**20),
    )(recv, query, columns, own, waves)


def per_device(proj, short_filter, skip_gain, norm_gain, filter_spectrum):
    chans, tok = proj.shape[1], proj.shape[2]
    peers = lax.axis_size("seq")
    groups = lax.axis_size("tp")
    waves = tables(peers, tok)
    taps = jnp.swapaxes(short_filter, 1, 2)
    sent, query, columns, own = pack(proj, filter_spectrum, taps, skip_gain[None], norm_gain[None])
    recv = lax.all_to_all(
        sent.reshape(peers, ROWS // 2, 2, tok), "seq", split_axis=0, concat_axis=0, tiled=True
    )
    recv = recv.reshape(peers * ROWS, tok)
    part, factor, gain = convolve(recv, query, columns, own, waves)
    part = lax.all_to_all(
        part.reshape(peers, 1, tok), "seq", split_axis=0, concat_axis=0, tiled=True
    )
    pre = part.reshape(chans, tok) * factor
    squares = lax.all_gather(jnp.sum(pre * pre, axis=0)[None], "tp", axis=0, tiled=True)
    meansq = jnp.sum(squares, axis=0) / (chans * groups)
    return (pre * lax.rsqrt(meansq + 1e-05)[None, :] * gain).astype(jnp.bfloat16)


def solution(mesh):
    return jax.shard_map(
        per_device,
        mesh=mesh,
        in_specs=(
            P(None, "tp", "seq"),
            P(None, "tp", None),
            P("tp"),
            P("tp"),
            P(None, "tp", "seq"),
        ),
        out_specs=P("tp", "seq"),
        check_vma=False,
    )
```

```python
import jax
import jax.numpy as jnp
import numpy as np
from jax import lax
from jax.experimental import pallas as pl
from jax.experimental.pallas import tpu as pltpu
from jax.sharding import PartitionSpec as P

ROWS = 6
EDGE_ROW = 5
SPARE = 16


def tables(n_coarse, n_fine):
    total = 2 * n_coarse * n_fine
    n1 = np.arange(n_coarse)
    k1 = np.arange(2 * n_coarse)
    n2 = np.arange(n_fine)
    turn = 2.0 * np.pi * (np.outer(n2, k1) % total) / total
    first = 2.0 * np.pi * (np.outer(n1, k1[:n_coarse]) % (2 * n_coarse)) / (2 * n_coarse)
    edge = np.concatenate([np.cos(first), -np.sin(first)], axis=1)
    inner = 2.0 * np.pi * (np.outer(n2, n2) % n_fine) / n_fine
    inner = np.concatenate([np.cos(inner), -np.sin(inner)], axis=1)
    fold = lambda x: np.concatenate([x[: len(x) // 2], x[len(x) // 2 :]], axis=1)
    turns = np.concatenate([np.cos(turn.T), -np.sin(turn.T)], axis=1)
    rows = [fold(edge), fold(inner), fold(turns), fold(fold(edge.T))]
    return jnp.asarray(np.concatenate(rows, axis=0), jnp.bfloat16)


def pack_kernel(
    proj_hbm, filt_hbm, taps_hbm, skip_hbm, gain_hbm,
    out_ref, query_ref, columns_ref, own_ref,
    proj_ref, filt_ref, taps_ref, small_ref, wide, sem_in, sem_small
):
    chans = proj_ref.shape[1]
    lanes = proj_ref.shape[2]
    small = [
        pltpu.make_async_copy(taps_hbm, taps_ref.at[pl.ds(0, 3)], sem_small.at[0]),
        pltpu.make_async_copy(skip_hbm, small_ref.at[pl.ds(9, 1)], sem_small.at[1]),
        pltpu.make_async_copy(gain_hbm, small_ref.at[pl.ds(10, 1)], sem_small.at[2]),
    ]
    proj_loads = [
        pltpu.make_async_copy(proj_hbm.at[:], proj_ref.at[:], sem_in.at[0, k])
        for k in range(1)
    ]
    filt_loads = [
        pltpu.make_async_copy(filt_hbm.at[k], filt_ref.at[k], sem_in.at[1, k])
        for k in range(2)
    ]
    for copy in small + proj_loads + filt_loads:
        copy.start()
    for copy in small:
        copy.wait()
    for i in range(3):
        small_ref[3 * i : 3 * i + 3, :] = taps_ref[i]
    lane = lax.broadcasted_iota(jnp.int32, (16, lanes), 1)
    param = lax.broadcasted_iota(jnp.int32, (16, lanes), 0)
    params = jnp.where(param < 11, small_ref[...], 0.0)
    columns = params.T
    columns_ref[...] = columns
    mine = jnp.where(lane == lax.axis_index("seq"), params, 0.0)
    own_ref[...] = jnp.broadcast_to(jnp.sum(mine, axis=1, keepdims=True), (16, lanes))
    lane = lax.broadcasted_iota(jnp.int32, (chans, lanes), 1)
    row = lambda r: pl.ds(r, chans, stride=ROWS)
    for copy in proj_loads:
        copy.wait()
    raw = [proj_ref[i].astype(jnp.float32) for i in range(3)]
    place = lax.broadcasted_iota(jnp.int32, (lanes, chans), 0)

    def conv(i):
        x = raw[i].T
        tap = lambda m: small_ref[3 * i + m : 3 * i + m + 1, :]
        late = tap(1) * jnp.where(place < 1, 0.0, pltpu.roll(x, 1, 0))
        return tap(0) * x + late + tap(2) * jnp.where(place < 2, 0.0, pltpu.roll(x, 2, 0))

    query_ref[...] = proj_ref[0]
    wide[row(0), :] = (conv(1) * conv(2)).T
    second = pltpu.roll(raw[2], 2, 1)
    fourth = pltpu.roll(raw[0], 4, 1)
    heads = jnp.where(lane < 2, raw[1], jnp.where(lane < 4, second, fourth))
    tails = jnp.where(lane < 2, second, jnp.where(lane < 4, fourth, raw[1]))
    wide[row(EDGE_ROW), :] = jnp.where(lane < 8, heads, pltpu.roll(tails, 10, 1))
    for copy in filt_loads:
        copy.wait()
    for part in range(2):
        for half in range(2):
            wide[row(1 + 2 * part + half), :] = filt_ref[
                part, :, lanes * half : lanes * (half + 1)
            ]
    out_ref[...] = wide[: chans * ROWS, :].astype(jnp.bfloat16)


def channel_kernel(
    recv_ref, query_ref, columns_ref, own_ref, waves_ref, out_ref, factor_ref, gain_ref, wide
):
    shards = out_ref.shape[0]
    lanes = out_ref.shape[1]
    size = 2 * shards
    wide[: shards * ROWS, :] = recv_ref[...].astype(jnp.float32)
    plane = lambda r: wide[pl.ds(r, shards, stride=ROWS), :]
    lane = lax.broadcasted_iota(jnp.int32, (shards, lanes), 1)
    shard = lax.broadcasted_iota(jnp.int32, (shards, lanes), 0)

    edges = plane(EDGE_ROW).T
    at = lax.broadcasted_iota(jnp.int32, (8, shards), 0)
    column = lax.broadcasted_iota(jnp.int32, (8, shards), 1)
    own = lambda p: own_ref[p : p + 1, :]
    tap = lambda m: jnp.where(at < 2, own(3 + m), jnp.where(at < 4, own(6 + m), own(m)))
    heads = edges[:8]
    two_ago = jnp.where(column == 0, 0.0, pltpu.roll(edges[8:16], 1, 1))
    one_ago = jnp.where(at % 2 == 1, pltpu.roll(heads, 1, 0), pltpu.roll(two_ago, 7, 0))
    conv = tap(0) * heads + tap(1) * one_ago + tap(2) * two_ago
    repair = (conv * pltpu.roll(conv, 6, 0)).astype(jnp.bfloat16).astype(jnp.float32)
    upright = plane(0).T
    mixed = jnp.concatenate([jnp.where(at < 2, repair, upright[:8]), upright[8:]], axis=0)
    rest = jnp.zeros((lanes - 8, shards), jnp.float32)
    spread = lambda x: jnp.concatenate([x, rest], axis=0).T
    skipped = own(9) * jnp.where(lane < 2, spread(repair), plane(0))
    query = spread(pltpu.roll(conv, 4, 0))

    unfold = lambda x: jnp.concatenate([x[:, :size], x[:, size:]], axis=0)
    square = lambda a, b, c, d: jnp.concatenate(
        [jnp.concatenate([a, b], axis=1), jnp.concatenate([c, d], axis=1)], axis=0
    )
    dot = lambda a, b, dims: lax.dot_general(
        a, b, (dims, ((), ())), preferred_element_type=jnp.float32
    )
    half = shards // 2
    edge = unfold(waves_ref[:half, :])
    flip = jnp.where(shard % 2 == 0, 1.0, -1.0).astype(jnp.bfloat16)
    c, d = edge[:, :shards], edge[:, shards:]
    edge = jnp.concatenate([c, c * flip, d, d * flip], axis=1)
    inner = unfold(waves_ref[half : half + lanes // 2, :])
    w_re, w_im = inner[:, :lanes], inner[:, lanes:]
    fwd, inv = square(w_re, w_im, -w_im, w_re), square(w_re, -w_im, w_im, w_re)
    turns = unfold(waves_ref[2 * half : 4 * half, :]).astype(jnp.float32)
    cos, sin = turns[:, :lanes], turns[:, lanes:]
    tall = unfold(waves_ref[4 * half :, :])
    tall = jnp.concatenate([tall[:, :shards], tall[:, shards:]], axis=0)
    flip = jnp.where(lane % 2 == 0, 1.0, -1.0).astype(jnp.bfloat16)
    c, d = tall[:shards], tall[shards:]
    tall = jnp.concatenate([c, c * flip, d, d * flip], axis=0)

    part = dot(tall, mixed.astype(jnp.bfloat16), ((1,), (1,)))
    a_re, a_im = part[:size], part[size:]
    b = jnp.concatenate([a_re * cos - a_im * sin, a_re * sin + a_im * cos], axis=1)
    spec = dot(b.astype(jnp.bfloat16), fwd, ((1,), (0,)))
    s_re, s_im = spec[:, :lanes], spec[:, lanes:]
    f_re = jnp.concatenate([plane(1).T, plane(2).T], axis=0)
    f_im = jnp.concatenate([plane(3).T, plane(4).T], axis=0)
    prod = jnp.concatenate([s_re * f_re - s_im * f_im, s_re * f_im + s_im * f_re], axis=1)
    time = dot(prod.astype(jnp.bfloat16), inv, ((1,), (0,)))
    c_re, c_im = time[:, :lanes], time[:, lanes:]
    d = jnp.concatenate([c_re * cos + c_im * sin, c_im * cos - c_re * sin], axis=0)
    long_out = dot(edge, d.astype(jnp.bfloat16), ((1,), (0,))) * (1.0 / (size * lanes))
    raw = query_ref[...].astype(jnp.float32)
    weight = lambda p: columns_ref[:, p : p + 1]
    gain_ref[...] = jnp.broadcast_to(weight(10), (shards, lanes))
    late = weight(1) * jnp.where(lane < 1, 0.0, pltpu.roll(raw, 1, 1))
    late = weight(0) * raw + late + weight(2) * jnp.where(lane < 2, 0.0, pltpu.roll(raw, 2, 1))
    factor_ref[...] = jnp.where(lane < 2, 1.0, late)
    both = long_out + skipped
    out_ref[...] = jnp.where(lane < 2, query * both, both)


def pack(proj, filter_spectrum, taps, skip, gain):
    chans, lanes = proj.shape[1], proj.shape[2]
    hbm = pl.BlockSpec(memory_space=pltpu.HBM)
    vmem = pl.BlockSpec(memory_space=pltpu.VMEM)
    inputs = (proj, filter_spectrum, taps, skip, gain)
    return pl.pallas_call(
        pack_kernel,
        out_shape=(
            jax.ShapeDtypeStruct((chans * ROWS, lanes), jnp.bfloat16),
            jax.ShapeDtypeStruct((chans, lanes), jnp.bfloat16),
            jax.ShapeDtypeStruct((chans, 16), jnp.float32),
            jax.ShapeDtypeStruct((16, lanes), jnp.float32),
        ),
        in_specs=[hbm] * len(inputs),
        out_specs=(vmem,) * 4,
        scratch_shapes=[
            pltpu.VMEM(proj.shape, proj.dtype),
            pltpu.VMEM(filter_spectrum.shape, filter_spectrum.dtype),
            pltpu.VMEM((6,) + taps.shape[1:], taps.dtype),
            pltpu.VMEM((16, lanes), jnp.float32),
            pltpu.VMEM((chans * ROWS + SPARE, lanes), jnp.float32),
            pltpu.SemaphoreType.DMA((2, 4)),
            pltpu.SemaphoreType.DMA((3,)),
        ],
        compiler_params=pltpu.CompilerParams(vmem_limit_bytes=16 * 2**20),
    )(*(pltpu.with_memory_space_constraint(x, pltpu.HBM) for x in inputs))


def convolve(recv, query, columns, own, waves):
    lanes = recv.shape[1]
    shards = recv.shape[0] // ROWS
    vmem = pl.BlockSpec(memory_space=pltpu.VMEM)
    return pl.pallas_call(
        channel_kernel,
        out_shape=(jax.ShapeDtypeStruct((shards, lanes), jnp.float32),) * 3,
        in_specs=[vmem] * 5,
        out_specs=(vmem,) * 3,
        scratch_shapes=[pltpu.VMEM((shards * ROWS + SPARE, lanes), jnp.float32)],
        compiler_params=pltpu.CompilerParams(vmem_limit_bytes=16 * 2**20),
    )(recv, query, columns, own, waves)


def per_device(proj, short_filter, skip_gain, norm_gain, filter_spectrum):
    chans, tok = proj.shape[1], proj.shape[2]
    peers = lax.axis_size("seq")
    groups = lax.axis_size("tp")
    waves = tables(peers, tok)
    taps = jnp.swapaxes(short_filter, 1, 2)
    sent, query, columns, own = pack(proj, filter_spectrum, taps, skip_gain[None], norm_gain[None])
    recv = lax.all_to_all(
        sent.reshape(peers, ROWS // 2, 2, tok), "seq", split_axis=0, concat_axis=0, tiled=True
    )
    recv = recv.reshape(peers * ROWS, tok)
    part, factor, gain = convolve(recv, query, columns, own, waves)
    part = lax.all_to_all(
        part.reshape(peers, 1, tok), "seq", split_axis=0, concat_axis=0, tiled=True
    )
    pre = part.reshape(chans, tok) * factor
    squares = lax.all_gather(jnp.sum(pre * pre, axis=0)[None], "tp", axis=0, tiled=True)
    meansq = jnp.sum(squares, axis=0) / (chans * groups)
    return (pre * lax.rsqrt(meansq + 1e-05)[None, :] * gain).astype(jnp.bfloat16)


def solution(mesh):
    return jax.shard_map(
        per_device,
        mesh=mesh,
        in_specs=(
            P(None, "tp", "seq"),
            P(None, "tp", None),
            P("tp"),
            P("tp"),
            P(None, "tp", "seq"),
        ),
        out_specs=P("tp", "seq"),
        check_vma=False,
    )
```

```python
import jax
import jax.numpy as jnp
import numpy as np
from jax import lax
from jax.experimental import pallas as pl
from jax.experimental.pallas import tpu as pltpu
from jax.sharding import PartitionSpec as P

ROWS = 6
EDGE_ROW = 5
SPARE = 16


def tables(n_coarse, n_fine):
    total = 2 * n_coarse * n_fine
    n1 = np.arange(n_coarse)
    k1 = np.arange(2 * n_coarse)
    n2 = np.arange(n_fine)
    turn = 2.0 * np.pi * (np.outer(n2, k1) % total) / total
    first = 2.0 * np.pi * (np.outer(n1, k1[:n_coarse]) % (2 * n_coarse)) / (2 * n_coarse)
    edge = np.concatenate([np.cos(first), -np.sin(first)], axis=1)
    inner = 2.0 * np.pi * (np.outer(n2, n2) % n_fine) / n_fine
    inner = np.concatenate([np.cos(inner), -np.sin(inner)], axis=1)
    fold = lambda x: np.concatenate([x[: len(x) // 2], x[len(x) // 2 :]], axis=1)
    turns = np.concatenate([np.cos(turn.T), -np.sin(turn.T)], axis=1)
    rows = [fold(edge), fold(inner), fold(turns), fold(fold(edge.T))]
    return jnp.asarray(np.concatenate(rows, axis=0), jnp.bfloat16)


def pack_kernel(
    proj_hbm, filt_hbm, taps_hbm, skip_hbm, gain_hbm,
    out_ref, query_ref, columns_ref, own_ref,
    proj_ref, filt_ref, taps_ref, small_ref, wide, sem_in, sem_small
):
    chans = proj_ref.shape[1]
    lanes = proj_ref.shape[2]
    small = [
        pltpu.make_async_copy(taps_hbm, taps_ref.at[pl.ds(0, 3)], sem_small.at[0]),
        pltpu.make_async_copy(skip_hbm, small_ref.at[pl.ds(9, 1)], sem_small.at[1]),
        pltpu.make_async_copy(gain_hbm, small_ref.at[pl.ds(10, 1)], sem_small.at[2]),
    ]
    proj_loads = [
        pltpu.make_async_copy(proj_hbm.at[:], proj_ref.at[:], sem_in.at[0, k])
        for k in range(1)
    ]
    filt_loads = [
        pltpu.make_async_copy(filt_hbm.at[k], filt_ref.at[k], sem_in.at[1, k])
        for k in range(2)
    ]
    for copy in small + proj_loads + filt_loads:
        copy.start()
    for copy in small:
        copy.wait()
    for i in range(3):
        small_ref[3 * i : 3 * i + 3, :] = taps_ref[i]
    lane = lax.broadcasted_iota(jnp.int32, (16, lanes), 1)
    param = lax.broadcasted_iota(jnp.int32, (16, lanes), 0)
    params = jnp.where(param < 11, small_ref[...], 0.0)
    columns = params.T
    columns_ref[...] = columns
    mine = jnp.where(lane == lax.axis_index("seq"), params, 0.0)
    own_ref[...] = jnp.broadcast_to(jnp.sum(mine, axis=1, keepdims=True), (16, lanes))
    lane = lax.broadcasted_iota(jnp.int32, (chans, lanes), 1)
    row = lambda r: pl.ds(r, chans, stride=ROWS)
    for copy in proj_loads:
        copy.wait()
    turned = [proj_ref[i].T.astype(jnp.float32) for i in range(3)]
    place = lax.broadcasted_iota(jnp.int32, (lanes, chans), 0)

    def conv(i):
        x = turned[i]
        tap = lambda m: small_ref[3 * i + m : 3 * i + m + 1, :]
        late = tap(1) * jnp.where(place < 1, 0.0, pltpu.roll(x, 1, 0))
        return tap(0) * x + late + tap(2) * jnp.where(place < 2, 0.0, pltpu.roll(x, 2, 0))

    query_ref[...] = proj_ref[0]
    wide[row(0), :] = (conv(1) * conv(2)).astype(jnp.bfloat16).T.astype(jnp.float32)
    at = lax.broadcasted_iota(jnp.int32, (8, chans), 0)
    q, k, v = ([x[:8], x[lanes - 8 :]] for x in turned)
    pick = lambda a, b, c: jnp.where(at < 2, a, jnp.where(at < 4, b, c))
    heads = pick(k[0], pltpu.roll(v[0], 2, 0), pltpu.roll(q[0], 4, 0))
    tails = pick(pltpu.roll(k[1], 2, 0), pltpu.roll(v[1], 4, 0), pltpu.roll(q[1], 6, 0))
    edges = jnp.concatenate([heads, tails, jnp.zeros((lanes - 16, chans), jnp.float32)], axis=0)
    wide[row(EDGE_ROW), :] = edges.astype(jnp.bfloat16).T.astype(jnp.float32)
    for copy in filt_loads:
        copy.wait()
    for part in range(2):
        for half in range(2):
            wide[row(1 + 2 * part + half), :] = filt_ref[
                part, :, lanes * half : lanes * (half + 1)
            ]
    out_ref[...] = wide[: chans * ROWS, :].astype(jnp.bfloat16)


def channel_kernel(
    recv_ref, query_ref, columns_ref, own_ref, waves_ref, out_ref, factor_ref, gain_ref, wide
):
    shards = out_ref.shape[0]
    lanes = out_ref.shape[1]
    size = 2 * shards
    wide[: shards * ROWS, :] = recv_ref[...].astype(jnp.float32)
    plane = lambda r: wide[pl.ds(r, shards, stride=ROWS), :]
    narrow = lambda r: plane(r).astype(jnp.bfloat16).T.astype(jnp.float32)
    lane = lax.broadcasted_iota(jnp.int32, (shards, lanes), 1)
    shard = lax.broadcasted_iota(jnp.int32, (shards, lanes), 0)

    edges = narrow(EDGE_ROW)
    at = lax.broadcasted_iota(jnp.int32, (8, shards), 0)
    column = lax.broadcasted_iota(jnp.int32, (8, shards), 1)
    own = lambda p: own_ref[p : p + 1, :]
    tap = lambda m: jnp.where(at < 2, own(3 + m), jnp.where(at < 4, own(6 + m), own(m)))
    heads = edges[:8]
    two_ago = jnp.where(column == 0, 0.0, pltpu.roll(edges[8:16], 1, 1))
    one_ago = jnp.where(at % 2 == 1, pltpu.roll(heads, 1, 0), pltpu.roll(two_ago, 7, 0))
    conv = tap(0) * heads + tap(1) * one_ago + tap(2) * two_ago
    repair = (conv * pltpu.roll(conv, 6, 0)).astype(jnp.bfloat16).astype(jnp.float32)
    upright = narrow(0)
    mixed = jnp.concatenate([jnp.where(at < 2, repair, upright[:8]), upright[8:]], axis=0)
    rest = jnp.zeros((lanes - 8, shards), jnp.float32)
    spread = lambda x: jnp.concatenate([x, rest], axis=0).T
    skipped = own(9) * jnp.where(lane < 2, spread(repair), plane(0))
    query = spread(pltpu.roll(conv, 4, 0))

    unfold = lambda x: jnp.concatenate([x[:, :size], x[:, size:]], axis=0)
    square = lambda a, b, c, d: jnp.concatenate(
        [jnp.concatenate([a, b], axis=1), jnp.concatenate([c, d], axis=1)], axis=0
    )
    dot = lambda a, b, dims: lax.dot_general(
        a, b, (dims, ((), ())), preferred_element_type=jnp.float32
    )
    half = shards // 2
    edge = unfold(waves_ref[:half, :])
    flip = jnp.where(shard % 2 == 0, 1.0, -1.0).astype(jnp.bfloat16)
    c, d = edge[:, :shards], edge[:, shards:]
    edge = jnp.concatenate([c, c * flip, d, d * flip], axis=1)
    inner = unfold(waves_ref[half : half + lanes // 2, :])
    w_re, w_im = inner[:, :lanes], inner[:, lanes:]
    fwd, inv = square(w_re, w_im, -w_im, w_re), square(w_re, -w_im, w_im, w_re)
    turns = unfold(waves_ref[2 * half : 4 * half, :]).astype(jnp.float32)
    cos, sin = turns[:, :lanes], turns[:, lanes:]
    tall = unfold(waves_ref[4 * half :, :])
    tall = jnp.concatenate([tall[:, :shards], tall[:, shards:]], axis=0)
    flip = jnp.where(lane % 2 == 0, 1.0, -1.0).astype(jnp.bfloat16)
    c, d = tall[:shards], tall[shards:]
    tall = jnp.concatenate([c, c * flip, d, d * flip], axis=0)

    part = dot(tall, mixed.astype(jnp.bfloat16), ((1,), (1,)))
    a_re, a_im = part[:size], part[size:]
    b = jnp.concatenate([a_re * cos - a_im * sin, a_re * sin + a_im * cos], axis=1)
    spec = dot(b.astype(jnp.bfloat16), fwd, ((1,), (0,)))
    s_re, s_im = spec[:, :lanes], spec[:, lanes:]
    f_re = jnp.concatenate([narrow(1), narrow(2)], axis=0)
    f_im = jnp.concatenate([narrow(3), narrow(4)], axis=0)
    prod = jnp.concatenate([s_re * f_re - s_im * f_im, s_re * f_im + s_im * f_re], axis=1)
    time = dot(prod.astype(jnp.bfloat16), inv, ((1,), (0,)))
    c_re, c_im = time[:, :lanes], time[:, lanes:]
    d = jnp.concatenate([c_re * cos + c_im * sin, c_im * cos - c_re * sin], axis=0)
    long_out = dot(edge, d.astype(jnp.bfloat16), ((1,), (0,))) * (1.0 / (size * lanes))
    raw = query_ref[...].astype(jnp.float32)
    weight = lambda p: columns_ref[:, p : p + 1]
    gain_ref[...] = jnp.broadcast_to(weight(10), (shards, lanes))
    late = weight(1) * jnp.where(lane < 1, 0.0, pltpu.roll(raw, 1, 1))
    late = weight(0) * raw + late + weight(2) * jnp.where(lane < 2, 0.0, pltpu.roll(raw, 2, 1))
    factor_ref[...] = jnp.where(lane < 2, 1.0, late)
    both = long_out + skipped
    out_ref[...] = jnp.where(lane < 2, query * both, both)


def pack(proj, filter_spectrum, taps, skip, gain):
    chans, lanes = proj.shape[1], proj.shape[2]
    hbm = pl.BlockSpec(memory_space=pltpu.HBM)
    vmem = pl.BlockSpec(memory_space=pltpu.VMEM)
    inputs = (proj, filter_spectrum, taps, skip, gain)
    return pl.pallas_call(
        pack_kernel,
        out_shape=(
            jax.ShapeDtypeStruct((chans * ROWS, lanes), jnp.bfloat16),
            jax.ShapeDtypeStruct((chans, lanes), jnp.bfloat16),
            jax.ShapeDtypeStruct((chans, 16), jnp.float32),
            jax.ShapeDtypeStruct((16, lanes), jnp.float32),
        ),
        in_specs=[hbm] * len(inputs),
        out_specs=(vmem,) * 4,
        scratch_shapes=[
            pltpu.VMEM(proj.shape, proj.dtype),
            pltpu.VMEM(filter_spectrum.shape, filter_spectrum.dtype),
            pltpu.VMEM((6,) + taps.shape[1:], taps.dtype),
            pltpu.VMEM((16, lanes), jnp.float32),
            pltpu.VMEM((chans * ROWS + SPARE, lanes), jnp.float32),
            pltpu.SemaphoreType.DMA((2, 4)),
            pltpu.SemaphoreType.DMA((3,)),
        ],
        compiler_params=pltpu.CompilerParams(vmem_limit_bytes=16 * 2**20),
    )(*(pltpu.with_memory_space_constraint(x, pltpu.HBM) for x in inputs))


def convolve(recv, query, columns, own, waves):
    lanes = recv.shape[1]
    shards = recv.shape[0] // ROWS
    vmem = pl.BlockSpec(memory_space=pltpu.VMEM)
    return pl.pallas_call(
        channel_kernel,
        out_shape=(jax.ShapeDtypeStruct((shards, lanes), jnp.float32),) * 3,
        in_specs=[vmem] * 5,
        out_specs=(vmem,) * 3,
        scratch_shapes=[pltpu.VMEM((shards * ROWS + SPARE, lanes), jnp.float32)],
        compiler_params=pltpu.CompilerParams(vmem_limit_bytes=16 * 2**20),
    )(recv, query, columns, own, waves)


def per_device(proj, short_filter, skip_gain, norm_gain, filter_spectrum):
    chans, tok = proj.shape[1], proj.shape[2]
    peers = lax.axis_size("seq")
    groups = lax.axis_size("tp")
    waves = tables(peers, tok)
    taps = jnp.swapaxes(short_filter, 1, 2)
    sent, query, columns, own = pack(proj, filter_spectrum, taps, skip_gain[None], norm_gain[None])
    recv = lax.all_to_all(
        sent.reshape(peers, ROWS // 2, 2, tok), "seq", split_axis=0, concat_axis=0, tiled=True
    )
    recv = recv.reshape(peers * ROWS, tok)
    part, factor, gain = convolve(recv, query, columns, own, waves)
    part = lax.all_to_all(
        part.reshape(peers, 1, tok), "seq", split_axis=0, concat_axis=0, tiled=True
    )
    pre = part.reshape(chans, tok) * factor
    squares = lax.all_gather(jnp.sum(pre * pre, axis=0)[None], "tp", axis=0, tiled=True)
    meansq = jnp.sum(squares, axis=0) / (chans * groups)
    return (pre * lax.rsqrt(meansq + 1e-05)[None, :] * gain).astype(jnp.bfloat16)


def solution(mesh):
    return jax.shard_map(
        per_device,
        mesh=mesh,
        in_specs=(
            P(None, "tp", "seq"),
            P(None, "tp", None),
            P("tp"),
            P("tp"),
            P(None, "tp", "seq"),
        ),
        out_specs=P("tp", "seq"),
        check_vma=False,
    )
```

```python
import jax
import jax.numpy as jnp
import numpy as np
from jax import lax
from jax.experimental import pallas as pl
from jax.experimental.pallas import tpu as pltpu
from jax.sharding import PartitionSpec as P

ROWS = 6
EDGE_ROW = 5
SPARE = 16


def tables(n_coarse, n_fine):
    total = 2 * n_coarse * n_fine
    n1 = np.arange(n_coarse)
    k1 = np.arange(2 * n_coarse)
    n2 = np.arange(n_fine)
    turn = 2.0 * np.pi * (np.outer(n2, k1) % total) / total
    first = 2.0 * np.pi * (np.outer(n1, k1[:n_coarse]) % (2 * n_coarse)) / (2 * n_coarse)
    edge = np.concatenate([np.cos(first), -np.sin(first)], axis=1)
    inner = 2.0 * np.pi * (np.outer(n2, n2) % n_fine) / n_fine
    inner = np.concatenate([np.cos(inner), -np.sin(inner)], axis=1)
    fold = lambda x: np.concatenate([x[: len(x) // 2], x[len(x) // 2 :]], axis=1)
    turns = np.concatenate([np.cos(turn.T), -np.sin(turn.T)], axis=1)
    rows = [fold(inner), fold(turns), fold(fold(edge.T))]
    return jnp.asarray(np.concatenate(rows, axis=0), jnp.bfloat16)


def pack_kernel(
    proj_hbm, filt_hbm, taps_hbm, skip_hbm, gain_hbm,
    out_ref, query_ref, columns_ref, own_ref,
    proj_ref, filt_ref, taps_ref, small_ref, wide, sem_in, sem_small
):
    chans = proj_ref.shape[1]
    lanes = proj_ref.shape[2]
    small = [
        pltpu.make_async_copy(taps_hbm, taps_ref.at[pl.ds(0, 3)], sem_small.at[0]),
        pltpu.make_async_copy(skip_hbm, small_ref.at[pl.ds(9, 1)], sem_small.at[1]),
        pltpu.make_async_copy(gain_hbm, small_ref.at[pl.ds(10, 1)], sem_small.at[2]),
    ]
    proj_loads = [
        pltpu.make_async_copy(proj_hbm.at[:], proj_ref.at[:], sem_in.at[0, k])
        for k in range(1)
    ]
    filt_loads = [
        pltpu.make_async_copy(filt_hbm.at[k], filt_ref.at[k], sem_in.at[1, k])
        for k in range(2)
    ]
    for copy in small + proj_loads + filt_loads:
        copy.start()
    for copy in small:
        copy.wait()
    for i in range(3):
        small_ref[3 * i : 3 * i + 3, :] = taps_ref[i]
    lane = lax.broadcasted_iota(jnp.int32, (16, lanes), 1)
    param = lax.broadcasted_iota(jnp.int32, (16, lanes), 0)
    params = jnp.where(param < 11, small_ref[...], 0.0)
    columns = params.T
    columns_ref[...] = columns
    mine = jnp.where(lane == lax.axis_index("seq"), params, 0.0)
    own_ref[...] = jnp.broadcast_to(jnp.sum(mine, axis=1, keepdims=True), (16, lanes))
    lane = lax.broadcasted_iota(jnp.int32, (chans, lanes), 1)
    row = lambda r: pl.ds(r, chans, stride=ROWS)
    for copy in proj_loads:
        copy.wait()
    turned = [proj_ref[i].T.astype(jnp.float32) for i in range(3)]
    place = lax.broadcasted_iota(jnp.int32, (lanes, chans), 0)

    def conv(i):
        x = turned[i]
        tap = lambda m: small_ref[3 * i + m : 3 * i + m + 1, :]
        late = tap(1) * jnp.where(place < 1, 0.0, pltpu.roll(x, 1, 0))
        return tap(0) * x + late + tap(2) * jnp.where(place < 2, 0.0, pltpu.roll(x, 2, 0))

    query_ref[...] = proj_ref[0]
    wide[row(0), :] = (conv(1) * conv(2)).astype(jnp.bfloat16).T.astype(jnp.float32)
    at = lax.broadcasted_iota(jnp.int32, (8, chans), 0)
    q, k, v = ([x[:8], x[lanes - 8 :]] for x in turned)
    pick = lambda a, b, c: jnp.where(at < 2, a, jnp.where(at < 4, b, c))
    heads = pick(k[0], pltpu.roll(v[0], 2, 0), pltpu.roll(q[0], 4, 0))
    tails = pick(pltpu.roll(k[1], 2, 0), pltpu.roll(v[1], 4, 0), pltpu.roll(q[1], 6, 0))
    edges = jnp.concatenate([heads, tails, jnp.zeros((lanes - 16, chans), jnp.float32)], axis=0)
    wide[row(EDGE_ROW), :] = edges.astype(jnp.bfloat16).T.astype(jnp.float32)
    for copy in filt_loads:
        copy.wait()
    for part in range(2):
        for half in range(2):
            wide[row(1 + 2 * part + half), :] = filt_ref[
                part, :, lanes * half : lanes * (half + 1)
            ]
    out_ref[...] = wide[: chans * ROWS, :].astype(jnp.bfloat16)


def channel_kernel(
    recv_ref, query_ref, columns_ref, own_ref, waves_ref, out_ref, factor_ref, gain_ref, wide
):
    shards = out_ref.shape[0]
    lanes = out_ref.shape[1]
    size = 2 * shards
    wide[: shards * ROWS, :] = recv_ref[...].astype(jnp.float32)
    plane = lambda r: wide[pl.ds(r, shards, stride=ROWS), :]
    narrow = lambda r: plane(r).astype(jnp.bfloat16).T.astype(jnp.float32)
    lane = lax.broadcasted_iota(jnp.int32, (shards, lanes), 1)
    shard = lax.broadcasted_iota(jnp.int32, (shards, lanes), 0)

    edges = narrow(EDGE_ROW)
    at = lax.broadcasted_iota(jnp.int32, (8, shards), 0)
    column = lax.broadcasted_iota(jnp.int32, (8, shards), 1)
    own = lambda p: own_ref[p : p + 1, :]
    tap = lambda m: jnp.where(at < 2, own(3 + m), jnp.where(at < 4, own(6 + m), own(m)))
    heads = edges[:8]
    two_ago = jnp.where(column == 0, 0.0, pltpu.roll(edges[8:16], 1, 1))
    one_ago = jnp.where(at % 2 == 1, pltpu.roll(heads, 1, 0), pltpu.roll(two_ago, 7, 0))
    conv = tap(0) * heads + tap(1) * one_ago + tap(2) * two_ago
    repair = (conv * pltpu.roll(conv, 6, 0)).astype(jnp.bfloat16).astype(jnp.float32)
    upright = narrow(0)
    mixed = jnp.concatenate([jnp.where(at < 2, repair, upright[:8]), upright[8:]], axis=0)
    rest = jnp.zeros((lanes - 8, shards), jnp.float32)
    spread = lambda x: jnp.concatenate([x, rest], axis=0).T
    skipped = own(9) * jnp.where(lane < 2, spread(repair), plane(0))
    query = spread(pltpu.roll(conv, 4, 0))

    unfold = lambda x: jnp.concatenate([x[:, :size], x[:, size:]], axis=0)
    square = lambda a, b, c, d: jnp.concatenate(
        [jnp.concatenate([a, b], axis=1), jnp.concatenate([c, d], axis=1)], axis=0
    )
    dot = lambda a, b, dims: lax.dot_general(
        a, b, (dims, ((), ())), preferred_element_type=jnp.float32
    )
    half = shards // 2
    inner = unfold(waves_ref[: lanes // 2, :])
    w_re, w_im = inner[:, :lanes], inner[:, lanes:]
    fwd, inv = square(w_re, w_im, -w_im, w_re), square(w_re, -w_im, w_im, w_re)
    turns = unfold(waves_ref[half : 3 * half, :]).astype(jnp.float32)
    cos, sin = turns[:, :lanes], turns[:, lanes:]
    tall = unfold(waves_ref[3 * half :, :])
    tall = jnp.concatenate([tall[:, :shards], tall[:, shards:]], axis=0)
    flip = jnp.where(lane % 2 == 0, 1.0, -1.0).astype(jnp.bfloat16)
    c, d = tall[:shards], tall[shards:]
    tall = jnp.concatenate([c, c * flip, d, d * flip], axis=0)
    edge = tall.T

    part = dot(tall, mixed.astype(jnp.bfloat16), ((1,), (1,)))
    a_re, a_im = part[:size], part[size:]
    b = jnp.concatenate([a_re * cos - a_im * sin, a_re * sin + a_im * cos], axis=1)
    spec = dot(b.astype(jnp.bfloat16), fwd, ((1,), (0,)))
    s_re, s_im = spec[:, :lanes], spec[:, lanes:]
    f_re = jnp.concatenate([narrow(1), narrow(2)], axis=0)
    f_im = jnp.concatenate([narrow(3), narrow(4)], axis=0)
    prod = jnp.concatenate([s_re * f_re - s_im * f_im, s_re * f_im + s_im * f_re], axis=1)
    time = dot(prod.astype(jnp.bfloat16), inv, ((1,), (0,)))
    c_re, c_im = time[:, :lanes], time[:, lanes:]
    d = jnp.concatenate([c_re * cos + c_im * sin, c_im * cos - c_re * sin], axis=0)
    long_out = dot(edge, d.astype(jnp.bfloat16), ((1,), (0,))) * (1.0 / (size * lanes))
    raw = query_ref[...].astype(jnp.float32)
    weight = lambda p: columns_ref[:, p : p + 1]
    gain_ref[...] = jnp.broadcast_to(weight(10), (shards, lanes))
    late = weight(1) * jnp.where(lane < 1, 0.0, pltpu.roll(raw, 1, 1))
    late = weight(0) * raw + late + weight(2) * jnp.where(lane < 2, 0.0, pltpu.roll(raw, 2, 1))
    factor_ref[...] = jnp.where(lane < 2, 1.0, late)
    both = long_out + skipped
    out_ref[...] = jnp.where(lane < 2, query * both, both)


def pack(proj, filter_spectrum, taps, skip, gain):
    chans, lanes = proj.shape[1], proj.shape[2]
    hbm = pl.BlockSpec(memory_space=pltpu.HBM)
    vmem = pl.BlockSpec(memory_space=pltpu.VMEM)
    inputs = (proj, filter_spectrum, taps, skip, gain)
    return pl.pallas_call(
        pack_kernel,
        out_shape=(
            jax.ShapeDtypeStruct((chans * ROWS, lanes), jnp.bfloat16),
            jax.ShapeDtypeStruct((chans, lanes), jnp.bfloat16),
            jax.ShapeDtypeStruct((chans, 16), jnp.float32),
            jax.ShapeDtypeStruct((16, lanes), jnp.float32),
        ),
        in_specs=[hbm] * len(inputs),
        out_specs=(vmem,) * 4,
        scratch_shapes=[
            pltpu.VMEM(proj.shape, proj.dtype),
            pltpu.VMEM(filter_spectrum.shape, filter_spectrum.dtype),
            pltpu.VMEM((6,) + taps.shape[1:], taps.dtype),
            pltpu.VMEM((16, lanes), jnp.float32),
            pltpu.VMEM((chans * ROWS + SPARE, lanes), jnp.float32),
            pltpu.SemaphoreType.DMA((2, 4)),
            pltpu.SemaphoreType.DMA((3,)),
        ],
        compiler_params=pltpu.CompilerParams(vmem_limit_bytes=16 * 2**20),
    )(*(pltpu.with_memory_space_constraint(x, pltpu.HBM) for x in inputs))


def convolve(recv, query, columns, own, waves):
    lanes = recv.shape[1]
    shards = recv.shape[0] // ROWS
    vmem = pl.BlockSpec(memory_space=pltpu.VMEM)
    return pl.pallas_call(
        channel_kernel,
        out_shape=(jax.ShapeDtypeStruct((shards, lanes), jnp.float32),) * 3,
        in_specs=[vmem] * 5,
        out_specs=(vmem,) * 3,
        scratch_shapes=[pltpu.VMEM((shards * ROWS + SPARE, lanes), jnp.float32)],
        compiler_params=pltpu.CompilerParams(vmem_limit_bytes=16 * 2**20),
    )(recv, query, columns, own, waves)


def per_device(proj, short_filter, skip_gain, norm_gain, filter_spectrum):
    chans, tok = proj.shape[1], proj.shape[2]
    peers = lax.axis_size("seq")
    groups = lax.axis_size("tp")
    waves = tables(peers, tok)
    taps = jnp.swapaxes(short_filter, 1, 2)
    sent, query, columns, own = pack(proj, filter_spectrum, taps, skip_gain[None], norm_gain[None])
    recv = lax.all_to_all(
        sent.reshape(peers, ROWS // 2, 2, tok), "seq", split_axis=0, concat_axis=0, tiled=True
    )
    recv = recv.reshape(peers * ROWS, tok)
    part, factor, gain = convolve(recv, query, columns, own, waves)
    part = lax.all_to_all(
        part.reshape(peers, 1, tok), "seq", split_axis=0, concat_axis=0, tiled=True
    )
    pre = part.reshape(chans, tok) * factor
    squares = lax.all_gather(jnp.sum(pre * pre, axis=0)[None], "tp", axis=0, tiled=True)
    meansq = jnp.sum(squares, axis=0) / (chans * groups)
    return (pre * lax.rsqrt(meansq + 1e-05)[None, :] * gain).astype(jnp.bfloat16)


def solution(mesh):
    return jax.shard_map(
        per_device,
        mesh=mesh,
        in_specs=(
            P(None, "tp", "seq"),
            P(None, "tp", None),
            P("tp"),
            P("tp"),
            P(None, "tp", "seq"),
        ),
        out_specs=P("tp", "seq"),
        check_vma=False,
    )
```

```python
import jax
import jax.numpy as jnp
import numpy as np
from jax import lax
from jax.experimental import pallas as pl
from jax.experimental.pallas import tpu as pltpu
from jax.sharding import PartitionSpec as P

ROWS = 6
EDGE_ROW = 5
SPARE = 16


def tables(n_coarse, n_fine):
    total = 2 * n_coarse * n_fine
    n1 = np.arange(n_coarse)
    k1 = np.arange(2 * n_coarse)
    n2 = np.arange(n_fine)
    turn = 2.0 * np.pi * (np.outer(n2, k1) % total) / total
    first = 2.0 * np.pi * (np.outer(n1, k1[:n_coarse]) % (2 * n_coarse)) / (2 * n_coarse)
    edge = np.concatenate([np.cos(first), -np.sin(first)], axis=1)
    inner = 2.0 * np.pi * (np.outer(n2, n2) % n_fine) / n_fine
    inner = np.concatenate([np.cos(inner), -np.sin(inner)], axis=1)
    fold = lambda x: np.concatenate([x[: len(x) // 2], x[len(x) // 2 :]], axis=1)
    turns = np.concatenate([np.cos(turn.T), -np.sin(turn.T)], axis=1)
    rows = [fold(inner), fold(turns), fold(fold(edge.T))]
    return jnp.asarray(np.concatenate(rows, axis=0), jnp.bfloat16)


def pack_kernel(
    proj_hbm, filt_hbm, taps_hbm, skip_hbm, gain_hbm,
    out_ref, query_ref, columns_ref, own_ref,
    proj_ref, filt_ref, taps_ref, small_ref, wide, sem_in, sem_small
):
    chans = proj_ref.shape[1]
    lanes = proj_ref.shape[2]
    small = [
        pltpu.make_async_copy(taps_hbm, taps_ref.at[pl.ds(0, 3)], sem_small.at[0]),
        pltpu.make_async_copy(skip_hbm, small_ref.at[pl.ds(9, 1)], sem_small.at[1]),
        pltpu.make_async_copy(gain_hbm, small_ref.at[pl.ds(10, 1)], sem_small.at[2]),
    ]
    proj_loads = [
        pltpu.make_async_copy(proj_hbm.at[:], proj_ref.at[:], sem_in.at[0, k])
        for k in range(1)
    ]
    filt_loads = [
        pltpu.make_async_copy(filt_hbm.at[k], filt_ref.at[k], sem_in.at[1, k])
        for k in range(2)
    ]
    for copy in small + proj_loads + filt_loads:
        copy.start()
    for copy in small:
        copy.wait()
    for i in range(3):
        small_ref[3 * i : 3 * i + 3, :] = taps_ref[i]
    lane = lax.broadcasted_iota(jnp.int32, (16, lanes), 1)
    param = lax.broadcasted_iota(jnp.int32, (16, lanes), 0)
    params = jnp.where(param < 11, small_ref[...], 0.0)
    columns = params.T
    columns_ref[...] = columns
    mine = jnp.where(lane == lax.axis_index("seq"), params, 0.0)
    own_ref[...] = jnp.broadcast_to(jnp.sum(mine, axis=1, keepdims=True), (16, lanes))
    lane = lax.broadcasted_iota(jnp.int32, (chans, lanes), 1)
    row = lambda r: pl.ds(r, chans, stride=ROWS)
    for copy in proj_loads:
        copy.wait()
    turned = [proj_ref[i].T.astype(jnp.float32) for i in range(3)]
    place = lax.broadcasted_iota(jnp.int32, (lanes, chans), 0)

    def conv(i):
        x = turned[i]
        tap = lambda m: small_ref[3 * i + m : 3 * i + m + 1, :]
        late = tap(1) * jnp.where(place < 1, 0.0, pltpu.roll(x, 1, 0))
        return tap(0) * x + late + tap(2) * jnp.where(place < 2, 0.0, pltpu.roll(x, 2, 0))

    query_ref[...] = proj_ref[0]
    wide[row(0), :] = (conv(1) * conv(2)).astype(jnp.bfloat16).T.astype(jnp.float32)
    at = lax.broadcasted_iota(jnp.int32, (8, chans), 0)
    q, k, v = ([x[:8], x[lanes - 8 :]] for x in turned)
    pick = lambda a, b, c: jnp.where(at < 2, a, jnp.where(at < 4, b, c))
    heads = pick(k[0], pltpu.roll(v[0], 2, 0), pltpu.roll(q[0], 4, 0))
    tails = pick(pltpu.roll(k[1], 2, 0), pltpu.roll(v[1], 4, 0), pltpu.roll(q[1], 6, 0))
    edges = jnp.concatenate([heads, tails, jnp.zeros((lanes - 16, chans), jnp.float32)], axis=0)
    wide[row(EDGE_ROW), :] = edges.astype(jnp.bfloat16).T.astype(jnp.float32)
    for copy in filt_loads:
        copy.wait()
    for part in range(2):
        for half in range(2):
            wide[row(1 + 2 * part + half), :] = filt_ref[
                part, :, lanes * half : lanes * (half + 1)
            ]
    out_ref[...] = wide[: chans * ROWS, :].astype(jnp.bfloat16)


def channel_kernel(
    recv_ref, query_ref, columns_ref, own_ref, waves_ref, out_ref, factor_ref, gain_ref, wide
):
    shards = out_ref.shape[0]
    lanes = out_ref.shape[1]
    size = 2 * shards
    wide[: shards * ROWS, :] = recv_ref[...].astype(jnp.float32)
    plane = lambda r: wide[pl.ds(r, shards, stride=ROWS), :]
    narrow = lambda r: plane(r).astype(jnp.bfloat16).T.astype(jnp.float32)
    lane = lax.broadcasted_iota(jnp.int32, (shards, lanes), 1)
    shard = lax.broadcasted_iota(jnp.int32, (shards, lanes), 0)

    edges = narrow(EDGE_ROW)
    at = lax.broadcasted_iota(jnp.int32, (8, shards), 0)
    column = lax.broadcasted_iota(jnp.int32, (8, shards), 1)
    own = lambda p: own_ref[p : p + 1, :]
    tap = lambda m: jnp.where(at < 2, own(3 + m), jnp.where(at < 4, own(6 + m), own(m)))
    heads = edges[:8]
    two_ago = jnp.where(column == 0, 0.0, pltpu.roll(edges[8:16], 1, 1))
    one_ago = jnp.where(at % 2 == 1, pltpu.roll(heads, 1, 0), pltpu.roll(two_ago, 7, 0))
    conv = tap(0) * heads + tap(1) * one_ago + tap(2) * two_ago
    repair = (conv * pltpu.roll(conv, 6, 0)).astype(jnp.bfloat16).astype(jnp.float32)
    upright = narrow(0)
    mixed = jnp.concatenate([jnp.where(at < 2, repair, upright[:8]), upright[8:]], axis=0)
    rest = jnp.zeros((lanes - 8, shards), jnp.float32)
    spread = lambda x: jnp.concatenate([x, rest], axis=0).T
    skipped = own(9) * jnp.where(lane < 2, spread(repair), plane(0))
    query = spread(pltpu.roll(conv, 4, 0))

    unfold = lambda x: jnp.concatenate([x[:, :size], x[:, size:]], axis=0)
    square = lambda a, b, c, d: jnp.concatenate(
        [jnp.concatenate([a, b], axis=1), jnp.concatenate([c, d], axis=1)], axis=0
    )
    dot = lambda a, b, dims: lax.dot_general(
        a, b, (dims, ((), ())), preferred_element_type=jnp.float32
    )
    half = shards // 2
    inner = unfold(waves_ref[: lanes // 2, :])
    w_re, w_im = inner[:, :lanes], inner[:, lanes:]
    fwd, inv = square(w_re, w_im, -w_im, w_re), square(w_re, -w_im, w_im, w_re)
    turns = unfold(waves_ref[half : 3 * half, :]).astype(jnp.float32)
    cos, sin = turns[:, :lanes], turns[:, lanes:]
    tall = unfold(waves_ref[3 * half :, :])
    tall = jnp.concatenate([tall[:, :shards], tall[:, shards:]], axis=0)
    flip = jnp.where(lane % 2 == 0, 1.0, -1.0).astype(jnp.bfloat16)
    c, d = tall[:shards], tall[shards:]
    tall = jnp.concatenate([c, c * flip, d, d * flip], axis=0)
    edge = tall.T

    part = dot(tall, mixed.astype(jnp.bfloat16), ((1,), (1,)))
    a_re, a_im = part[:size], part[size:]
    b = jnp.concatenate([a_re * cos - a_im * sin, a_re * sin + a_im * cos], axis=1)
    spec = dot(b.astype(jnp.bfloat16), fwd, ((1,), (0,)))
    s_re, s_im = spec[:, :lanes], spec[:, lanes:]
    f_re = jnp.concatenate([narrow(1), narrow(2)], axis=0)
    f_im = jnp.concatenate([narrow(3), narrow(4)], axis=0)
    prod = jnp.concatenate([s_re * f_re - s_im * f_im, s_re * f_im + s_im * f_re], axis=1)
    time = dot(prod.astype(jnp.bfloat16), inv, ((1,), (0,)))
    c_re, c_im = time[:, :lanes], time[:, lanes:]
    d = jnp.concatenate([c_re * cos + c_im * sin, c_im * cos - c_re * sin], axis=0)
    long_out = dot(edge, d.astype(jnp.bfloat16), ((1,), (0,))) * (1.0 / (size * lanes))
    raw = query_ref[...].astype(jnp.float32)
    weight = lambda p: columns_ref[:, p : p + 1]
    gain_ref[...] = jnp.broadcast_to(weight(10), (shards, lanes))
    late = weight(1) * jnp.where(lane < 1, 0.0, pltpu.roll(raw, 1, 1))
    late = weight(0) * raw + late + weight(2) * jnp.where(lane < 2, 0.0, pltpu.roll(raw, 2, 1))
    factor_ref[...] = jnp.where(lane < 2, 1.0, late)
    both = long_out + skipped
    out_ref[...] = jnp.where(lane < 2, query * both, both)


def pack(proj, filter_spectrum, taps, skip, gain):
    chans, lanes = proj.shape[1], proj.shape[2]
    hbm = pl.BlockSpec(memory_space=pltpu.HBM)
    vmem = pl.BlockSpec(memory_space=pltpu.VMEM)
    inputs = (proj, filter_spectrum, taps, skip, gain)
    return pl.pallas_call(
        pack_kernel,
        out_shape=(
            jax.ShapeDtypeStruct((chans * ROWS, lanes), jnp.bfloat16),
            jax.ShapeDtypeStruct((chans, lanes), jnp.bfloat16),
            jax.ShapeDtypeStruct((chans, 16), jnp.float32),
            jax.ShapeDtypeStruct((16, lanes), jnp.float32),
        ),
        in_specs=[hbm] * len(inputs),
        out_specs=(vmem,) * 4,
        scratch_shapes=[
            pltpu.VMEM(proj.shape, proj.dtype),
            pltpu.VMEM(filter_spectrum.shape, filter_spectrum.dtype),
            pltpu.VMEM((6,) + taps.shape[1:], taps.dtype),
            pltpu.VMEM((16, lanes), jnp.float32),
            pltpu.VMEM((chans * ROWS + SPARE, lanes), jnp.float32),
            pltpu.SemaphoreType.DMA((2, 4)),
            pltpu.SemaphoreType.DMA((3,)),
        ],
        compiler_params=pltpu.CompilerParams(vmem_limit_bytes=16 * 2**20),
    )(*(pltpu.with_memory_space_constraint(x, pltpu.HBM) for x in inputs))


def convolve(recv, query, columns, own, waves):
    lanes = recv.shape[1]
    shards = recv.shape[0] // ROWS
    vmem = pl.BlockSpec(memory_space=pltpu.VMEM)
    return pl.pallas_call(
        channel_kernel,
        out_shape=(jax.ShapeDtypeStruct((shards, lanes), jnp.float32),) * 3,
        in_specs=[vmem] * 5,
        out_specs=(vmem,) * 3,
        scratch_shapes=[pltpu.VMEM((shards * ROWS + SPARE, lanes), jnp.float32)],
        compiler_params=pltpu.CompilerParams(vmem_limit_bytes=16 * 2**20),
    )(recv, query, columns, own, waves)


def per_device(proj, short_filter, skip_gain, norm_gain, filter_spectrum):
    chans, tok = proj.shape[1], proj.shape[2]
    peers = lax.axis_size("seq")
    groups = lax.axis_size("tp")
    waves = tables(peers, tok)
    taps = jnp.swapaxes(short_filter, 1, 2)
    sent, query, columns, own = pack(proj, filter_spectrum, taps, skip_gain[None], norm_gain[None])
    recv = lax.all_to_all(
        sent.reshape(peers, ROWS // 2, 2, tok), "seq", split_axis=0, concat_axis=0, tiled=True
    )
    recv = recv.reshape(peers * ROWS, tok)
    part, factor, gain = convolve(recv, query, columns, own, waves)
    part = lax.all_to_all(
        part.reshape(peers, 1, tok), "seq", split_axis=0, concat_axis=0, tiled=True
    )
    pre = part.reshape(chans, tok) * factor
    squares = jnp.broadcast_to(jnp.sum(pre * pre, axis=0)[None, None], (groups, 1, tok))
    squares = lax.all_to_all(squares, "tp", split_axis=0, concat_axis=0, tiled=True)
    meansq = jnp.sum(squares[:, 0], axis=0) / (chans * groups)
    return (pre * lax.rsqrt(meansq + 1e-05)[None, :] * gain).astype(jnp.bfloat16)


def solution(mesh):
    return jax.shard_map(
        per_device,
        mesh=mesh,
        in_specs=(
            P(None, "tp", "seq"),
            P(None, "tp", None),
            P("tp"),
            P("tp"),
            P(None, "tp", "seq"),
        ),
        out_specs=P("tp", "seq"),
        check_vma=False,
    )
```

```python
import jax
import jax.numpy as jnp
import numpy as np
from jax import lax
from jax.experimental import pallas as pl
from jax.experimental.pallas import tpu as pltpu
from jax.sharding import PartitionSpec as P

ROWS = 6
EDGE_ROW = 5
SPARE = 16


def tables(n_coarse, n_fine):
    total = 2 * n_coarse * n_fine
    n1 = np.arange(n_coarse)
    k1 = np.arange(2 * n_coarse)
    n2 = np.arange(n_fine)
    turn = 2.0 * np.pi * (np.outer(n2, k1) % total) / total
    first = 2.0 * np.pi * (np.outer(n1, k1[:n_coarse]) % (2 * n_coarse)) / (2 * n_coarse)
    edge = np.concatenate([np.cos(first), -np.sin(first)], axis=1)
    inner = 2.0 * np.pi * (np.outer(n2, n2) % n_fine) / n_fine
    inner = np.concatenate([np.cos(inner), -np.sin(inner)], axis=1)
    fold = lambda x: np.concatenate([x[: len(x) // 2], x[len(x) // 2 :]], axis=1)
    turns = np.concatenate([np.cos(turn.T), -np.sin(turn.T)], axis=1)
    rows = [fold(inner), fold(turns), fold(fold(edge.T))]
    return jnp.asarray(np.concatenate(rows, axis=0), jnp.bfloat16)


def pack_kernel(
    proj_hbm, filt_hbm, taps_hbm, skip_hbm, gain_hbm,
    out_ref, query_ref, columns_ref, own_ref,
    proj_ref, filt_ref, taps_ref, small_ref, wide, sem_in, sem_small
):
    chans = proj_ref.shape[1]
    lanes = proj_ref.shape[2]
    small = [
        pltpu.make_async_copy(taps_hbm, taps_ref.at[pl.ds(0, 3)], sem_small.at[0]),
        pltpu.make_async_copy(skip_hbm, small_ref.at[pl.ds(9, 1)], sem_small.at[1]),
        pltpu.make_async_copy(gain_hbm, small_ref.at[pl.ds(10, 1)], sem_small.at[2]),
    ]
    proj_loads = [
        pltpu.make_async_copy(proj_hbm.at[:], proj_ref.at[:], sem_in.at[0, k])
        for k in range(1)
    ]
    filt_loads = [
        pltpu.make_async_copy(filt_hbm.at[k], filt_ref.at[k], sem_in.at[1, k])
        for k in range(2)
    ]
    for copy in small + proj_loads + filt_loads:
        copy.start()
    for copy in small:
        copy.wait()
    for i in range(3):
        small_ref[3 * i : 3 * i + 3, :] = taps_ref[i]
    lane = lax.broadcasted_iota(jnp.int32, (16, lanes), 1)
    param = lax.broadcasted_iota(jnp.int32, (16, lanes), 0)
    params = jnp.where(param < 11, small_ref[...], 0.0)
    columns = params.T
    columns_ref[...] = columns
    mine = jnp.where(lane == lax.axis_index("seq"), params, 0.0)
    own_ref[...] = jnp.broadcast_to(jnp.sum(mine, axis=1, keepdims=True), (16, lanes))
    lane = lax.broadcasted_iota(jnp.int32, (chans, lanes), 1)
    row = lambda r: pl.ds(r, chans, stride=ROWS)
    for copy in proj_loads:
        copy.wait()
    turned = [proj_ref[i].T.astype(jnp.float32) for i in range(3)]
    place = lax.broadcasted_iota(jnp.int32, (lanes, chans), 0)

    def conv(i):
        x = turned[i]
        tap = lambda m: small_ref[3 * i + m : 3 * i + m + 1, :]
        late = tap(1) * jnp.where(place < 1, 0.0, pltpu.roll(x, 1, 0))
        return tap(0) * x + late + tap(2) * jnp.where(place < 2, 0.0, pltpu.roll(x, 2, 0))

    query_ref[...] = proj_ref[0]
    wide[row(0), :] = (conv(1) * conv(2)).astype(jnp.bfloat16).T.astype(jnp.float32)
    at = lax.broadcasted_iota(jnp.int32, (8, chans), 0)
    q, k, v = ([x[:8], x[lanes - 8 :]] for x in turned)
    pick = lambda a, b, c: jnp.where(at < 2, a, jnp.where(at < 4, b, c))
    heads = pick(k[0], pltpu.roll(v[0], 2, 0), pltpu.roll(q[0], 4, 0))
    tails = pick(pltpu.roll(k[1], 2, 0), pltpu.roll(v[1], 4, 0), pltpu.roll(q[1], 6, 0))
    odd = at % 2 == 1
    own_ago = jnp.where(odd, pltpu.roll(heads, 1, 0), 0.0)
    past_ago = jnp.where(odd, 0.0, pltpu.roll(tails, 7, 0))
    spare = jnp.zeros((lanes - 32, chans), jnp.float32)
    edges = jnp.concatenate([heads, tails, own_ago, past_ago, spare], axis=0)
    wide[row(EDGE_ROW), :] = edges.astype(jnp.bfloat16).T.astype(jnp.float32)
    for copy in filt_loads:
        copy.wait()
    for part in range(2):
        for half in range(2):
            wide[row(1 + 2 * part + half), :] = filt_ref[
                part, :, lanes * half : lanes * (half + 1)
            ]
    out_ref[...] = wide[: chans * ROWS, :].astype(jnp.bfloat16)


def channel_kernel(
    recv_ref, query_ref, columns_ref, own_ref, waves_ref, out_ref, factor_ref, gain_ref, wide
):
    shards = out_ref.shape[0]
    lanes = out_ref.shape[1]
    size = 2 * shards
    wide[: shards * ROWS, :] = recv_ref[...].astype(jnp.float32)
    plane = lambda r: wide[pl.ds(r, shards, stride=ROWS), :]
    narrow = lambda r: plane(r).astype(jnp.bfloat16).T.astype(jnp.float32)
    lane = lax.broadcasted_iota(jnp.int32, (shards, lanes), 1)
    shard = lax.broadcasted_iota(jnp.int32, (shards, lanes), 0)

    edges = narrow(EDGE_ROW)
    at = lax.broadcasted_iota(jnp.int32, (8, shards), 0)
    column = lax.broadcasted_iota(jnp.int32, (8, shards), 1)
    own = lambda p: own_ref[p : p + 1, :]
    tap = lambda m: jnp.where(at < 2, own(3 + m), jnp.where(at < 4, own(6 + m), own(m)))
    heads = edges[:8]
    two_ago = jnp.where(column == 0, 0.0, pltpu.roll(edges[8:16], 1, 1))
    past_ago = jnp.where(column == 0, 0.0, pltpu.roll(edges[24:32], 1, 1))
    one_ago = edges[16:24] + past_ago
    conv = tap(0) * heads + tap(1) * one_ago + tap(2) * two_ago
    repair = (conv * pltpu.roll(conv, 6, 0)).astype(jnp.bfloat16).astype(jnp.float32)
    upright = narrow(0)
    mixed = jnp.concatenate([jnp.where(at < 2, repair, upright[:8]), upright[8:]], axis=0)
    rest = jnp.zeros((lanes - 8, shards), jnp.float32)
    spread = lambda x: jnp.concatenate([x, rest], axis=0).T
    skipped = own(9) * jnp.where(lane < 2, spread(repair), plane(0))
    query = spread(pltpu.roll(conv, 4, 0))

    unfold = lambda x: jnp.concatenate([x[:, :size], x[:, size:]], axis=0)
    square = lambda a, b, c, d: jnp.concatenate(
        [jnp.concatenate([a, b], axis=1), jnp.concatenate([c, d], axis=1)], axis=0
    )
    dot = lambda a, b, dims: lax.dot_general(
        a, b, (dims, ((), ())), preferred_element_type=jnp.float32
    )
    half = shards // 2
    inner = unfold(waves_ref[: lanes // 2, :])
    w_re, w_im = inner[:, :lanes], inner[:, lanes:]
    fwd, inv = square(w_re, w_im, -w_im, w_re), square(w_re, -w_im, w_im, w_re)
    turns = unfold(waves_ref[half : 3 * half, :]).astype(jnp.float32)
    cos, sin = turns[:, :lanes], turns[:, lanes:]
    tall = unfold(waves_ref[3 * half :, :])
    tall = jnp.concatenate([tall[:, :shards], tall[:, shards:]], axis=0)
    flip = jnp.where(lane % 2 == 0, 1.0, -1.0).astype(jnp.bfloat16)
    c, d = tall[:shards], tall[shards:]
    tall = jnp.concatenate([c, c * flip, d, d * flip], axis=0)
    edge = tall.T

    part = dot(tall, mixed.astype(jnp.bfloat16), ((1,), (1,)))
    a_re, a_im = part[:size], part[size:]
    b = jnp.concatenate([a_re * cos - a_im * sin, a_re * sin + a_im * cos], axis=1)
    spec = dot(b.astype(jnp.bfloat16), fwd, ((1,), (0,)))
    s_re, s_im = spec[:, :lanes], spec[:, lanes:]
    f_re = jnp.concatenate([narrow(1), narrow(2)], axis=0)
    f_im = jnp.concatenate([narrow(3), narrow(4)], axis=0)
    prod = jnp.concatenate([s_re * f_re - s_im * f_im, s_re * f_im + s_im * f_re], axis=1)
    time = dot(prod.astype(jnp.bfloat16), inv, ((1,), (0,)))
    c_re, c_im = time[:, :lanes], time[:, lanes:]
    d = jnp.concatenate([c_re * cos + c_im * sin, c_im * cos - c_re * sin], axis=0)
    long_out = dot(edge, d.astype(jnp.bfloat16), ((1,), (0,))) * (1.0 / (size * lanes))
    raw = query_ref[...].astype(jnp.float32)
    weight = lambda p: columns_ref[:, p : p + 1]
    gain_ref[...] = jnp.broadcast_to(weight(10), (shards, lanes))
    late = weight(1) * jnp.where(lane < 1, 0.0, pltpu.roll(raw, 1, 1))
    late = weight(0) * raw + late + weight(2) * jnp.where(lane < 2, 0.0, pltpu.roll(raw, 2, 1))
    factor_ref[...] = jnp.where(lane < 2, 1.0, late)
    both = long_out + skipped
    out_ref[...] = jnp.where(lane < 2, query * both, both)


def pack(proj, filter_spectrum, taps, skip, gain):
    chans, lanes = proj.shape[1], proj.shape[2]
    hbm = pl.BlockSpec(memory_space=pltpu.HBM)
    vmem = pl.BlockSpec(memory_space=pltpu.VMEM)
    inputs = (proj, filter_spectrum, taps, skip, gain)
    return pl.pallas_call(
        pack_kernel,
        out_shape=(
            jax.ShapeDtypeStruct((chans * ROWS, lanes), jnp.bfloat16),
            jax.ShapeDtypeStruct((chans, lanes), jnp.bfloat16),
            jax.ShapeDtypeStruct((chans, 16), jnp.float32),
            jax.ShapeDtypeStruct((16, lanes), jnp.float32),
        ),
        in_specs=[hbm] * len(inputs),
        out_specs=(vmem,) * 4,
        scratch_shapes=[
            pltpu.VMEM(proj.shape, proj.dtype),
            pltpu.VMEM(filter_spectrum.shape, filter_spectrum.dtype),
            pltpu.VMEM((6,) + taps.shape[1:], taps.dtype),
            pltpu.VMEM((16, lanes), jnp.float32),
            pltpu.VMEM((chans * ROWS + SPARE, lanes), jnp.float32),
            pltpu.SemaphoreType.DMA((2, 4)),
            pltpu.SemaphoreType.DMA((3,)),
        ],
        compiler_params=pltpu.CompilerParams(vmem_limit_bytes=16 * 2**20),
    )(*(pltpu.with_memory_space_constraint(x, pltpu.HBM) for x in inputs))


def convolve(recv, query, columns, own, waves):
    lanes = recv.shape[1]
    shards = recv.shape[0] // ROWS
    vmem = pl.BlockSpec(memory_space=pltpu.VMEM)
    return pl.pallas_call(
        channel_kernel,
        out_shape=(jax.ShapeDtypeStruct((shards, lanes), jnp.float32),) * 3,
        in_specs=[vmem] * 5,
        out_specs=(vmem,) * 3,
        scratch_shapes=[pltpu.VMEM((shards * ROWS + SPARE, lanes), jnp.float32)],
        compiler_params=pltpu.CompilerParams(vmem_limit_bytes=16 * 2**20),
    )(recv, query, columns, own, waves)


def per_device(proj, short_filter, skip_gain, norm_gain, filter_spectrum):
    chans, tok = proj.shape[1], proj.shape[2]
    peers = lax.axis_size("seq")
    groups = lax.axis_size("tp")
    waves = tables(peers, tok)
    taps = jnp.swapaxes(short_filter, 1, 2)
    sent, query, columns, own = pack(proj, filter_spectrum, taps, skip_gain[None], norm_gain[None])
    recv = lax.all_to_all(
        sent.reshape(peers, ROWS // 2, 2, tok), "seq", split_axis=0, concat_axis=0, tiled=True
    )
    recv = recv.reshape(peers * ROWS, tok)
    part, factor, gain = convolve(recv, query, columns, own, waves)
    part = lax.all_to_all(
        part.reshape(peers, 1, tok), "seq", split_axis=0, concat_axis=0, tiled=True
    )
    pre = part.reshape(chans, tok) * factor
    squares = jnp.broadcast_to(jnp.sum(pre * pre, axis=0)[None, None], (groups, 1, tok))
    squares = lax.all_to_all(squares, "tp", split_axis=0, concat_axis=0, tiled=True)
    meansq = jnp.sum(squares[:, 0], axis=0) / (chans * groups)
    return (pre * lax.rsqrt(meansq + 1e-05)[None, :] * gain).astype(jnp.bfloat16)


def solution(mesh):
    return jax.shard_map(
        per_device,
        mesh=mesh,
        in_specs=(
            P(None, "tp", "seq"),
            P(None, "tp", None),
            P("tp"),
            P("tp"),
            P(None, "tp", "seq"),
        ),
        out_specs=P("tp", "seq"),
        check_vma=False,
    )
```

```python
import jax
import jax.numpy as jnp
import numpy as np
from jax import lax
from jax.experimental import pallas as pl
from jax.experimental.pallas import tpu as pltpu
from jax.sharding import PartitionSpec as P

ROWS = 6
EDGE_ROW = 5
SPARE = 16


def tables(n_coarse, n_fine):
    total = 2 * n_coarse * n_fine
    n1 = np.arange(n_coarse)
    k1 = np.arange(2 * n_coarse)
    n2 = np.arange(n_fine)
    turn = 2.0 * np.pi * (np.outer(n2, k1) % total) / total
    first = 2.0 * np.pi * (np.outer(n1, k1[:n_coarse]) % (2 * n_coarse)) / (2 * n_coarse)
    edge = np.concatenate([np.cos(first), -np.sin(first)], axis=1)
    inner = 2.0 * np.pi * (np.outer(n2, n2) % n_fine) / n_fine
    inner = np.concatenate([np.cos(inner), -np.sin(inner)], axis=1)
    fold = lambda x: np.concatenate([x[: len(x) // 2], x[len(x) // 2 :]], axis=1)
    turns = np.concatenate([np.cos(turn.T), -np.sin(turn.T)], axis=1)
    rows = [fold(inner), fold(turns), fold(fold(edge.T))]
    return jnp.asarray(np.concatenate(rows, axis=0), jnp.bfloat16)


def pack_kernel(
    proj_hbm, filt_hbm, taps_hbm, skip_hbm, gain_hbm,
    out_ref, query_ref, columns_ref, own_ref,
    proj_ref, filt_ref, taps_ref, small_ref, wide, sem_in, sem_small
):
    chans = proj_ref.shape[1]
    lanes = proj_ref.shape[2]
    small = [
        pltpu.make_async_copy(taps_hbm, taps_ref.at[pl.ds(0, 3)], sem_small.at[0]),
        pltpu.make_async_copy(skip_hbm, small_ref.at[pl.ds(9, 1)], sem_small.at[1]),
        pltpu.make_async_copy(gain_hbm, small_ref.at[pl.ds(10, 1)], sem_small.at[2]),
    ]
    proj_loads = [
        pltpu.make_async_copy(proj_hbm.at[:], proj_ref.at[:], sem_in.at[0, k])
        for k in range(1)
    ]
    filt_loads = [
        pltpu.make_async_copy(filt_hbm.at[k], filt_ref.at[k], sem_in.at[1, k])
        for k in range(2)
    ]
    for copy in small + proj_loads + filt_loads:
        copy.start()
    for copy in small:
        copy.wait()
    for i in range(3):
        small_ref[3 * i : 3 * i + 3, :] = taps_ref[i]
    lane = lax.broadcasted_iota(jnp.int32, (16, lanes), 1)
    param = lax.broadcasted_iota(jnp.int32, (16, lanes), 0)
    params = jnp.where(param < 11, small_ref[...], 0.0)
    columns = params.T
    columns_ref[...] = columns
    mine = jnp.where(lane == lax.axis_index("seq"), params, 0.0)
    own_ref[...] = jnp.broadcast_to(jnp.sum(mine, axis=1, keepdims=True), (16, lanes))
    lane = lax.broadcasted_iota(jnp.int32, (chans, lanes), 1)
    row = lambda r: pl.ds(r, chans, stride=ROWS)
    for copy in proj_loads:
        copy.wait()
    turned = [proj_ref[i].T.astype(jnp.float32) for i in range(3)]
    place = lax.broadcasted_iota(jnp.int32, (lanes, chans), 0)

    def conv(i):
        x = turned[i]
        tap = lambda m: small_ref[3 * i + m : 3 * i + m + 1, :]
        late = tap(1) * jnp.where(place < 1, 0.0, pltpu.roll(x, 1, 0))
        return tap(0) * x + late + tap(2) * jnp.where(place < 2, 0.0, pltpu.roll(x, 2, 0))

    query_ref[...] = proj_ref[0]
    wide[row(0), :] = (conv(1) * conv(2)).astype(jnp.bfloat16).T.astype(jnp.float32)
    at = lax.broadcasted_iota(jnp.int32, (8, chans), 0)
    q, k, v = ([x[:8], x[lanes - 8 :]] for x in turned)
    pick = lambda a, b, c: jnp.where(at < 2, a, jnp.where(at < 4, b, c))
    heads = pick(k[0], pltpu.roll(v[0], 2, 0), pltpu.roll(q[0], 4, 0))
    tails = pick(pltpu.roll(k[1], 2, 0), pltpu.roll(v[1], 4, 0), pltpu.roll(q[1], 6, 0))
    edges = jnp.concatenate([heads, tails, jnp.zeros((lanes - 16, chans), jnp.float32)], axis=0)
    wide[row(EDGE_ROW), :] = edges.astype(jnp.bfloat16).T.astype(jnp.float32)
    for copy in filt_loads:
        copy.wait()
    for part in range(2):
        for half in range(2):
            wide[row(1 + 2 * part + half), :] = filt_ref[
                part, :, lanes * half : lanes * (half + 1)
            ]
    out_ref[...] = wide[: chans * ROWS, :].astype(jnp.bfloat16)


def channel_kernel(
    recv_ref, query_ref, columns_ref, own_ref, waves_ref, out_ref, factor_ref, gain_ref, wide
):
    shards = out_ref.shape[0]
    lanes = out_ref.shape[1]
    size = 2 * shards
    wide[: shards * ROWS, :] = recv_ref[...].astype(jnp.float32)
    plane = lambda r: wide[pl.ds(r, shards, stride=ROWS), :]
    narrow = lambda r: plane(r).astype(jnp.bfloat16).T.astype(jnp.float32)
    lane = lax.broadcasted_iota(jnp.int32, (shards, lanes), 1)
    shard = lax.broadcasted_iota(jnp.int32, (shards, lanes), 0)

    edges = narrow(EDGE_ROW)
    at = lax.broadcasted_iota(jnp.int32, (8, shards), 0)
    column = lax.broadcasted_iota(jnp.int32, (8, shards), 1)
    own = lambda p: own_ref[p : p + 1, :]
    tap = lambda m: jnp.where(at < 2, own(3 + m), jnp.where(at < 4, own(6 + m), own(m)))
    heads = edges[:8]
    two_ago = jnp.where(column == 0, 0.0, pltpu.roll(edges[8:16], 1, 1))
    one_ago = jnp.where(at % 2 == 1, pltpu.roll(heads, 1, 0), pltpu.roll(two_ago, 7, 0))
    conv = tap(0) * heads + tap(1) * one_ago + tap(2) * two_ago
    repair = (conv * pltpu.roll(conv, 6, 0)).astype(jnp.bfloat16).astype(jnp.float32)
    upright = narrow(0)
    mixed = jnp.concatenate([jnp.where(at < 2, repair, upright[:8]), upright[8:]], axis=0)
    rest = jnp.zeros((lanes - 8, shards), jnp.float32)
    spread = lambda x: jnp.concatenate([x, rest], axis=0).T
    skipped = own(9) * jnp.where(lane < 2, spread(repair), plane(0))
    query = spread(pltpu.roll(conv, 4, 0))

    unfold = lambda x: jnp.concatenate([x[:, :size], x[:, size:]], axis=0)
    square = lambda a, b, c, d: jnp.concatenate(
        [jnp.concatenate([a, b], axis=1), jnp.concatenate([c, d], axis=1)], axis=0
    )
    dot = lambda a, b, dims: lax.dot_general(
        a, b, (dims, ((), ())), preferred_element_type=jnp.float32
    )
    half = shards // 2
    inner = unfold(waves_ref[: lanes // 2, :])
    w_re, w_im = inner[:, :lanes], inner[:, lanes:]
    fwd = square(w_re, w_im, -w_im, w_re)
    scale = jnp.asarray(1.0 / (size * lanes), jnp.bfloat16)
    w_re, w_im = w_re * scale, w_im * scale
    inv = square(w_re, -w_im, w_im, w_re)
    turns = unfold(waves_ref[half : 3 * half, :]).astype(jnp.float32)
    cos, sin = turns[:, :lanes], turns[:, lanes:]
    tall = unfold(waves_ref[3 * half :, :])
    tall = jnp.concatenate([tall[:, :shards], tall[:, shards:]], axis=0)
    flip = jnp.where(lane % 2 == 0, 1.0, -1.0).astype(jnp.bfloat16)
    c, d = tall[:shards], tall[shards:]
    tall = jnp.concatenate([c, c * flip, d, d * flip], axis=0)
    edge = tall.T

    part = dot(tall, mixed.astype(jnp.bfloat16), ((1,), (1,)))
    a_re, a_im = part[:size], part[size:]
    b = jnp.concatenate([a_re * cos - a_im * sin, a_re * sin + a_im * cos], axis=1)
    spec = dot(b.astype(jnp.bfloat16), fwd, ((1,), (0,)))
    s_re, s_im = spec[:, :lanes], spec[:, lanes:]
    f_re = jnp.concatenate([narrow(1), narrow(2)], axis=0)
    f_im = jnp.concatenate([narrow(3), narrow(4)], axis=0)
    prod = jnp.concatenate([s_re * f_re - s_im * f_im, s_re * f_im + s_im * f_re], axis=1)
    time = dot(prod.astype(jnp.bfloat16), inv, ((1,), (0,)))
    c_re, c_im = time[:, :lanes], time[:, lanes:]
    d = jnp.concatenate([c_re * cos + c_im * sin, c_im * cos - c_re * sin], axis=0)
    long_out = dot(edge, d.astype(jnp.bfloat16), ((1,), (0,)))
    raw = query_ref[...].astype(jnp.float32)
    weight = lambda p: columns_ref[:, p : p + 1]
    gain_ref[...] = jnp.broadcast_to(weight(10), (shards, lanes))
    late = weight(1) * jnp.where(lane < 1, 0.0, pltpu.roll(raw, 1, 1))
    late = weight(0) * raw + late + weight(2) * jnp.where(lane < 2, 0.0, pltpu.roll(raw, 2, 1))
    factor_ref[...] = jnp.where(lane < 2, 1.0, late)
    both = long_out + skipped
    out_ref[...] = jnp.where(lane < 2, query * both, both)


def pack(proj, filter_spectrum, taps, skip, gain):
    chans, lanes = proj.shape[1], proj.shape[2]
    hbm = pl.BlockSpec(memory_space=pltpu.HBM)
    vmem = pl.BlockSpec(memory_space=pltpu.VMEM)
    inputs = (proj, filter_spectrum, taps, skip, gain)
    return pl.pallas_call(
        pack_kernel,
        out_shape=(
            jax.ShapeDtypeStruct((chans * ROWS, lanes), jnp.bfloat16),
            jax.ShapeDtypeStruct((chans, lanes), jnp.bfloat16),
            jax.ShapeDtypeStruct((chans, 16), jnp.float32),
            jax.ShapeDtypeStruct((16, lanes), jnp.float32),
        ),
        in_specs=[hbm] * len(inputs),
        out_specs=(vmem,) * 4,
        scratch_shapes=[
            pltpu.VMEM(proj.shape, proj.dtype),
            pltpu.VMEM(filter_spectrum.shape, filter_spectrum.dtype),
            pltpu.VMEM((6,) + taps.shape[1:], taps.dtype),
            pltpu.VMEM((16, lanes), jnp.float32),
            pltpu.VMEM((chans * ROWS + SPARE, lanes), jnp.float32),
            pltpu.SemaphoreType.DMA((2, 4)),
            pltpu.SemaphoreType.DMA((3,)),
        ],
        compiler_params=pltpu.CompilerParams(vmem_limit_bytes=16 * 2**20),
    )(*(pltpu.with_memory_space_constraint(x, pltpu.HBM) for x in inputs))


def convolve(recv, query, columns, own, waves):
    lanes = recv.shape[1]
    shards = recv.shape[0] // ROWS
    vmem = pl.BlockSpec(memory_space=pltpu.VMEM)
    return pl.pallas_call(
        channel_kernel,
        out_shape=(jax.ShapeDtypeStruct((shards, lanes), jnp.float32),) * 3,
        in_specs=[vmem] * 5,
        out_specs=(vmem,) * 3,
        scratch_shapes=[pltpu.VMEM((shards * ROWS + SPARE, lanes), jnp.float32)],
        compiler_params=pltpu.CompilerParams(vmem_limit_bytes=16 * 2**20),
    )(recv, query, columns, own, waves)


def per_device(proj, short_filter, skip_gain, norm_gain, filter_spectrum):
    chans, tok = proj.shape[1], proj.shape[2]
    peers = lax.axis_size("seq")
    groups = lax.axis_size("tp")
    waves = tables(peers, tok)
    taps = jnp.swapaxes(short_filter, 1, 2)
    sent, query, columns, own = pack(proj, filter_spectrum, taps, skip_gain[None], norm_gain[None])
    recv = lax.all_to_all(
        sent.reshape(peers, ROWS // 2, 2, tok), "seq", split_axis=0, concat_axis=0, tiled=True
    )
    recv = recv.reshape(peers * ROWS, tok)
    part, factor, gain = convolve(recv, query, columns, own, waves)
    part = lax.all_to_all(
        part.reshape(peers, 1, tok), "seq", split_axis=0, concat_axis=0, tiled=True
    )
    pre = part.reshape(chans, tok) * factor
    squares = jnp.broadcast_to(jnp.sum(pre * pre, axis=0)[None, None], (groups, 1, tok))
    squares = lax.all_to_all(squares, "tp", split_axis=0, concat_axis=0, tiled=True)
    meansq = jnp.sum(squares[:, 0], axis=0) / (chans * groups)
    return (pre * lax.rsqrt(meansq + 1e-05)[None, :] * gain).astype(jnp.bfloat16)


def solution(mesh):
    return jax.shard_map(
        per_device,
        mesh=mesh,
        in_specs=(
            P(None, "tp", "seq"),
            P(None, "tp", None),
            P("tp"),
            P("tp"),
            P(None, "tp", "seq"),
        ),
        out_specs=P("tp", "seq"),
        check_vma=False,
    )
```
